512 devices in a mesh: dp: 32 (over z, x), expert: 16 (over y, core).
Axes of the slice: x: 4, y: 8, z: 8, core: 2. Of those that a mesh axis runs over, the one named last changes fastest.
Arguments:
- tokens: bfloat16 [1024, 3072], P(('dp', 'expert')), may hold values from -6 to 6
- cotangent: bfloat16 [1024, 3072], P(('dp', 'expert')), may hold values from -6 to 6
- route_ids: int32 [1024, 4], P(('dp', 'expert')), may hold values from 0 to 15, all different within a row; in each aligned block of 32 rows (0 to 31, 32 to 63, ...) at most 16 rows name the same one
- gate_probs: float32 [1024, 4], P(('dp', 'expert')), may hold values from 0.05 to 1
- w_gate: bfloat16 [16, 3072, 5376], P('expert', None, 'dp'), may hold values from -0.109375 to 0.109375
- w_up: bfloat16 [16, 3072, 5376], P('expert', None, 'dp'), may hold values from -0.109375 to 0.109375
- w_down: bfloat16 [16, 5376, 3072], P('expert', 'dp'), may hold values from -0.078125 to 0.078125
Outputs:
- token_grad: bfloat16 [1024, 3072], P(('dp', 'expert'))
- down_grad: bfloat16 [16, 5376, 3072], P('expert', 'dp')
The draws below stay inside these ranges and needn't reach their ends.
Inputs may be any that keep to these rules, and one draw needn't show every extreme that they name: `route_ids`: each row names 4 different experts. In each aligned block of 32 rows (the tokens of one index of dp) no expert is named by more than 16 rows, a bound that some block reaches.
All inputs are finite; a program needn't handle non-finite values.
Results may differ from the reference program's by a relative error of at most 0.023.
Values may be sent and summed in bfloat16 or wider, within the bound.
A program may use at most 64 MiB of HBM per device.

```python
import math
import jax
import jax.numpy as jnp
import numpy as np
from jax import lax

D = 3072
FF = 5376
TOPK = 4
TOK_DEV = 2
EXPERTS = 16
LOAD = 16
TOKENS = 1024
N_DP = 32
N_EXPERT = 16


def level_of(stream_key, extent, shards, least, top_value):
    def one(axis_at, parts):
        heights = jax.random.uniform(jax.random.fold_in(jax.random.fold_in(stream_key, 6), axis_at), (parts,), jnp.float32, least / len(shards), top_value / len(shards))
        return jnp.repeat(jnp.exp(heights), extent[axis_at] // parts).reshape((-1,) + (1,) * (len(extent) - axis_at - 1))

    gain = one(*shards[0])
    for cut in shards[1:]:
        gain = gain * one(*cut)
    return gain


def shared_out(key, own, number, rows, amount, top, bound, lean):
    ranking = jax.random.permutation(key, amount)
    packed, ordinary = load_shares(amount, rows * top, bound, lean, True), load_shares(amount, rows * top, bound, lean, False)
    places = jnp.arange(amount)

    def named(sizes, rotation):
        used = int((sizes > 0).sum())
        fixed = max(1, used // 4)
        shifted = fixed + (places - fixed + rotation * (used - fixed)) % max(1, amount - fixed)
        return jnp.zeros((amount,), jnp.int32).at[ranking[jnp.where(places < fixed, places, shifted)]].set(jnp.asarray(sizes, jnp.int32))

    sizes = jnp.where(number % 4 == 0, named(packed, number // 4), named(ordinary, number - number // 4 - 1))
    mixed = jax.random.permutation(jax.random.fold_in(own, 3), amount)
    donor, sink = mixed[0:amount // 2 * 2:2], mixed[1:amount // 2 * 2:2]
    margin = jnp.minimum(sizes[donor] - 1, bound - sizes[sink]) // 2
    margin = jnp.where((donor == ranking[0]) | (sink == ranking[0]) | (sizes[sink] == 0), 0, jnp.maximum(margin, 0))
    shifted = jax.random.randint(jax.random.fold_in(own, 4), (amount // 2,), 0, 1 << 20) % (margin + 1)
    sizes = sizes.at[donor].add(-shifted).at[sink].add(shifted)
    members = jnp.searchsorted(jnp.cumsum(sizes), jnp.arange(rows * top), side="right").astype(jnp.int32)
    grid = members.reshape(top, rows).T
    grid = grid[jax.random.permutation(jax.random.fold_in(own, 1), rows)]
    rotation = jax.random.randint(jax.random.fold_in(own, 2), (rows, 1), 0, top)
    return jnp.take_along_axis(grid, (jnp.arange(top)[None, :] + rotation) % top, axis=1)


def load_shares(amount, total, reach, lean, full):
    portions = [(1 << 20) // math.isqrt(rank ** lean) + 1 for rank in range(1, amount + 1)]
    largest = reach if full else min(reach, max(-(-total // amount), total * portions[0] // sum(portions)))
    least = 1 if total - largest >= amount - 1 else 0
    given, surplus = [largest] + [least] * (amount - 1), total - largest - least * (amount - 1)
    while surplus > 0:
        free = [i for i in range(1, amount) if given[i] < largest] or [i for i in range(1, amount) if given[i] < reach]
        pool, budget = sum([portions[i] for i in free]), surplus
        for i in free:
            addition = min(reach - given[i], max(1, budget * portions[i] // pool), surplus)
            given[i] = given[i] + addition
            surplus = surplus - addition
    return np.array(given)


def centred(key, dims, spread, most, pieces=(), held_as=jnp.bfloat16):
    drawn = spread * jax.random.normal(key, dims, jnp.float32)
    if pieces:
        drawn = drawn * level_of(key, dims, pieces, -0.22, 0.18)
    return jnp.clip(drawn, -most, most).astype(held_as)


def setup_inputs(seed: int = 0) -> dict:
    seeds = jax.random.split(jax.random.key(seed), 8)
    tokens = centred(seeds[0], (TOKENS, D), 1.0, 6.0, ((0, 512),))
    cotangent = centred(seeds[1], (TOKENS, D), 1.0, 6.0, ((0, 512),))
    route_ids_keys = jax.random.split(jax.random.fold_in(seeds[2], 1), TOKENS // (TOK_DEV * N_EXPERT))
    route_ids_turns = jax.random.permutation(jax.random.fold_in(seeds[2], 3), TOKENS // (TOK_DEV * N_EXPERT))
    route_ids = jax.vmap(lambda own, number: shared_out(jax.random.fold_in(seeds[2], 2), own, number, TOK_DEV * N_EXPERT, EXPERTS, TOPK, LOAD, 2))(route_ids_keys, route_ids_turns).reshape((TOKENS, TOPK))
    gate_probs = jnp.clip(jnp.exp(math.log(1.0) - 2.9957323 * jax.random.uniform(seeds[3], (TOKENS, TOPK), jnp.float32) ** level_of(seeds[3], (TOKENS, TOPK), ((0, 512),), -0.2, 0.2)), 0.05, 1.0)
    w_gate = centred(seeds[4], (EXPERTS, D, FF), D ** -0.5, 0.109375, ((0, 16), (2, 32)))
    w_up = centred(seeds[5], (EXPERTS, D, FF), D ** -0.5, 0.109375, ((0, 16), (2, 32)))
    w_down = centred(seeds[6], (EXPERTS, FF, D), FF ** -0.5, 0.078125, ((0, 16), (1, 32)))
    return {"tokens": tokens, "cotangent": cotangent, "route_ids": route_ids, "gate_probs": gate_probs, "w_gate": w_gate, "w_up": w_up, "w_down": w_down}


def silu_parts(gate_pre):
    sigma = jax.nn.sigmoid(gate_pre)
    return gate_pre * sigma, sigma * (1.0 + gate_pre * (1.0 - sigma))


def reference(tokens, cotangent, route_ids, gate_probs, w_gate, w_up, w_down):
    row_cap = N_DP * LOAD
    group = FF // N_DP

    def one_expert(grad_total, inputs):
        gate_mat, up_mat, down_mat, expert_id = inputs
        chosen = route_ids == expert_id
        routed = jnp.any(chosen, axis=1)
        weight = jnp.sum(jnp.where(chosen, gate_probs, 0.0), axis=1)
        index = jnp.nonzero(routed, size=row_cap, fill_value=0)[0].astype(jnp.int32)
        live = jnp.arange(row_cap, dtype=jnp.int32) < jnp.sum(routed.astype(jnp.int32))
        rows_in = jnp.where(live[:, None], tokens[index], jnp.zeros((), jnp.bfloat16))
        scaled = weight[index][:, None] * cotangent[index].astype(jnp.float32)
        rows_grad = jnp.where(live[:, None], scaled, 0.0).astype(jnp.bfloat16)
        gate_pre = jnp.dot(rows_in, gate_mat, preferred_element_type=jnp.float32)
        up_pre = jnp.dot(rows_in, up_mat, preferred_element_type=jnp.float32)
        active, slope_term = silu_parts(gate_pre)
        hidden = (active * up_pre).astype(jnp.bfloat16)
        hidden_grad = jnp.dot(rows_grad, down_mat.T, preferred_element_type=jnp.float32)
        gate_grad = (hidden_grad * up_pre * slope_term).astype(jnp.bfloat16)
        up_grad = (hidden_grad * active).astype(jnp.bfloat16)
        down_part = jnp.dot(hidden.T, rows_grad, preferred_element_type=jnp.float32).astype(jnp.bfloat16)

        def add_group(step, total):
            start = (step * group).astype(jnp.int32)
            gate_cols = lax.dynamic_slice_in_dim(gate_grad, start, group, 1)
            up_cols = lax.dynamic_slice_in_dim(up_grad, start, group, 1)
            gate_rows = lax.dynamic_slice_in_dim(gate_mat, start, group, 1)
            up_rows = lax.dynamic_slice_in_dim(up_mat, start, group, 1)
            part = jnp.dot(gate_cols, gate_rows.T, preferred_element_type=jnp.float32)
            part = part + jnp.dot(up_cols, up_rows.T, preferred_element_type=jnp.float32)
            rounded = lax.optimization_barrier(part.astype(jnp.bfloat16))
            return total + rounded.astype(jnp.float32)

        summed = lax.fori_loop(0, N_DP, add_group, jnp.zeros((row_cap, D), jnp.float32))
        route_grad = summed.astype(jnp.bfloat16).astype(jnp.float32)
        route_grad = jnp.where(live[:, None], route_grad, 0.0)
        grad_total = grad_total.at[index].add(route_grad)
        return grad_total, down_part

    start_total = jnp.zeros((TOKENS, D), jnp.float32)
    expert_list = jnp.arange(EXPERTS, dtype=jnp.int32)
    grad_total, down_grad = lax.scan(one_expert, start_total, (w_gate, w_up, w_down, expert_list))
    return grad_total.astype(jnp.bfloat16), down_grad
```

```python
import functools

import jax
import jax.numpy as jnp
import numpy as np
from jax import lax
from jax.experimental import pallas as pl
from jax.experimental.pallas import tpu as pltpu
from jax.sharding import PartitionSpec as P

MESH = pl.DeviceIdType.MESH
F32 = jnp.float32
BF16 = jnp.bfloat16
PIECES = 3
ROWS = 16
LANES = 128
SEGS = 8
WIDE = SEGS * LANES
ORDERS = (("x", "y", "z"), ("y", "z", "x"), ("z", "x", "y"))
META = 3


def nearest(n):
    return sorted(range(1, n), key=lambda r: min(r, n - r))


def rows_of(value):
    return value.reshape(-1, value.shape[-1])


class Grid:
    def __init__(self, sizes):
        self.n = sizes
        dp, ex = lax.axis_index("dp"), lax.axis_index("expert")
        self.at = {"z": dp // sizes["x"], "x": dp % sizes["x"], "y": ex // 2}
        self.core = ex % 2
        self.sign = 1 - 2 * self.core

    def device(self, axis=None, steps=0):
        at = dict(self.at)
        core = self.core
        if axis is None:
            core = 1 - core
        else:
            n = self.n[axis]
            at[axis] = (at[axis] + self.sign * steps + n) % n
        return (at["z"] * self.n["x"] + at["x"], at["y"] * 2 + core)


def kernel(
    sizes, block_ref, meta_ref, wg_hbm, wu_hbm, wd_hbm, fore_ref, back_ref, place_ref,
    out_ref, dg_ref,
    blocks0, blocks1, blocks2, metas, xt, xc, wg, wu, wd, weights, gate, up, grad,
    hidden, ggrad, ugrad, route0, route1, route2, sib0, sib1, sib2, land0, land1, land2,
    once0, once1, once2, near0, near1, near2, twice0, twice1, twice2, last0, last1, last2,
    load_sem, g1_send, g1_recv, g2_send, g2_recv, g3_send, g3_recv, s_send, s_recv,
    e_send, e_recv, a_send, a_recv, b_send, b_recv, c_send, c_recv,
):
    grid = Grid(sizes)
    nz, nx, ny = sizes["z"], sizes["x"], sizes["y"]
    other = grid.device()

    barrier = pltpu.get_barrier_semaphore()
    around = [other]
    for axis in ("x", "y", "z"):
        around += [grid.device(axis, r) for r in range(1, sizes[axis])]
    for device in around:
        pl.semaphore_signal(barrier, inc=1, device_id=device, device_id_type=MESH)

    loads = [
        pltpu.make_async_copy(src, dst, load_sem.at[i])
        for i, (src, dst) in enumerate(((wg_hbm, wg), (wu_hbm, wu), (wd_hbm, wd)))
    ]
    for load in loads:
        load.start()

    refs = (blocks0, blocks1, blocks2, metas)
    for p in range(PIECES):
        refs[p][0, 0, 0, 0] = block_ref[p]
    metas[0, 0, 0, 0] = meta_ref[...]
    pl.semaphore_wait(barrier, len(around))

    pending = []

    def push(src, dst, ssem, rsem, device):
        copy = pltpu.make_async_remote_copy(
            src_ref=src, dst_ref=dst, send_sem=ssem, recv_sem=rsem,
            device_id=device, device_id_type=MESH,
        )
        copy.start()
        pending.append(copy)

    def arrived(dst, ssem, rsem):
        pltpu.make_async_remote_copy(
            src_ref=dst, dst_ref=dst, send_sem=ssem, recv_sem=rsem,
            device_id=other, device_id_type=MESH,
        ).wait_recv()

    streams = []
    for q, ref in enumerate(refs):
        order = ORDERS[1 if q == META else q]
        streams.append((ref, order, tuple(sizes[a] for a in order)))
    for q, (ref, order, (n1, n2, n3)) in enumerate(streams):
        for r in nearest(n1):
            push(ref.at[0, 0, 0, 0], ref.at[0, 0, 0, n1 - r], g1_send.at[q, r],
                 g1_recv.at[q, n1 - r], grid.device(order[0], r))
    for q, (ref, order, (n1, n2, n3)) in enumerate(streams):
        for r in range(1, n1):
            arrived(ref.at[0, 0, 0, r], g1_send.at[q, r], g1_recv.at[q, r])
        for r in nearest(n2):
            push(ref.at[0, 0, 0], ref.at[0, 0, n2 - r], g2_send.at[q, r],
                 g2_recv.at[q, n2 - r], grid.device(order[1], r))

    def parts_of(q):
        return 1 if q == META else 4

    def turns_of(q):
        return (0,) if q == META else (0, 3, 1, 2)

    have = [{0} for _ in streams]

    def part(ref, lead, q, h):
        n2 = streams[q][2][1]
        size = n2 // parts_of(q)
        return ref.at[lead + (pl.ds(h * size, size),)]

    def share(q, slot):
        ref = refs[q]
        push(ref.at[0, slot], ref.at[1, slot], s_send.at[q, slot], s_recv.at[q, slot], other)

    def shared(q, slot):
        arrived(refs[q].at[1, slot], s_send.at[q, slot], s_recv.at[q, slot])

    def landed(q, way, k, i):
        n3 = streams[q][2][2]
        slot = n3 - k if way == 0 else k
        sem = (q, way, (k - 1) * parts_of(q) + i)
        arrived(part(refs[q], (0, slot), q, turns_of(q)[i]), g3_send.at[sem], g3_recv.at[sem])
        if i == parts_of(q) - 1:
            share(q, slot)

    def hop(q, k, i):
        ref, order, (n1, n2, n3) = streams[q]
        h = turns_of(q)[i]
        if k == 1:
            size = n2 // parts_of(q)
            for r in range(h * size, (h + 1) * size):
                if r not in have[q]:
                    arrived(ref.at[0, 0, r], g2_send.at[q, r], g2_recv.at[q, r])
                    have[q].add(r)
        for way in (0, 1):
            if k > n3 // 2 - way:
                continue
            if k > 1:
                landed(q, way, k - 1, i)
            src = (n3 - (k - 1)) % n3 if way == 0 else k - 1
            dst = n3 - k if way == 0 else k
            sem = (q, way, (k - 1) * parts_of(q) + i)
            push(part(ref, (0, src), q, h), part(ref, (0, dst), q, h), g3_send.at[sem],
                 g3_recv.at[sem], grid.device(order[2], 1 if way == 0 else -1))
        if k == 1 and i == parts_of(q) - 1:
            share(q, 0)

    def spread(p, box, tiles):
        held = box[...]
        tok = held[..., :ROWS, :].reshape(-1, LANES)
        cot = held[..., ROWS:, :].reshape(-1, LANES)
        both = jnp.concatenate([tok, cot], axis=1)
        moved = jnp.dot(fore_ref[p], both, preferred_element_type=F32).astype(BF16)
        for s in range(SEGS):
            columns = slice(p * WIDE + s * LANES, p * WIDE + (s + 1) * LANES)
            for t, tile in enumerate(tiles):
                start = (s * 2 + t) * ROWS
                xt[tile + (slice(None), columns)] = moved[start:start + ROWS, :LANES]
                xc[tile + (slice(None), columns)] = moved[start:start + ROWS, LANES:]

    across = (((1,), (1,)), ((), ()))

    def multiply(p, where):
        columns = slice(p * WIDE, (p + 1) * WIDE)
        tok = rows_of(xt[where + (slice(None), columns)])
        cot = rows_of(xc[where + (slice(None), columns)])
        for acc, lhs, w in ((gate, tok, wg), (up, tok, wu), (grad, cot, wd)):
            add = lax.dot_general(lhs, w[:, columns], across, preferred_element_type=F32)
            old = acc[where]
            acc[where] = old + add.reshape(old.shape)

    everything = slice(None)

    def take0(zi):
        for slot in (2 * zi, 2 * zi + 1):
            shared(0, slot)

        def body(i, _):
            c, yi = i // (ny // 2), i % (ny // 2)
            spread(0, blocks0.at[c, pl.ds(2 * zi, 2), pl.ds(2 * yi, 2)],
                   [(c, zi, yi, 0), (c, zi, yi, 1)])
            return 0

        lax.fori_loop(0, ny, body, 0)
        multiply(0, (everything, zi, everything, everything))

    def take2(yi):
        for slot in (2 * yi, 2 * yi + 1):
            shared(2, slot)

        def body(i, _):
            c, zi = i // (nz // 2), i % (nz // 2)
            spread(2, blocks2.at[c, pl.ds(2 * yi, 2), :, pl.ds(2 * zi, 2)],
                   [(c, zi, yi, 0), (c, zi, yi, 1)])
            return 0

        lax.fori_loop(0, nz, body, 0)
        multiply(2, (everything, everything, yi, everything))

    def take1(xi):
        for slot in (2 * xi, 2 * xi + 1):
            shared(1, slot)
        quads = ny // 4

        def body(i, _):
            c, rest = i // (nz // 2 * quads), i % (nz // 2 * quads)
            zi, yq = rest // quads, rest % quads
            spread(1, blocks1.at[c, pl.ds(2 * xi, 2), pl.ds(2 * zi, 2), pl.ds(4 * yq, 4)],
                   [(c, zi, 2 * yq, xi), (c, zi, 2 * yq + 1, xi)])
            return 0

        lax.fori_loop(0, nz * quads, body, 0)

        def each(c, _):
            multiply(1, (c, everything, everything, xi))
            return 0

        lax.fori_loop(0, 2, each, 0)

    gate[...] = jnp.zeros_like(gate)
    up[...] = jnp.zeros_like(up)
    grad[...] = jnp.zeros_like(grad)

    hops = max(nz, ny) // 2
    items = 4 * hops
    done = {0: set(), 1: set(), 2: set()}

    def complete(q, k):
        n3 = streams[q][2][2]
        return {0} | {n3 - j for j in range(1, k + 1)} | {j for j in range(1, min(k, n3 // 2 - 1) + 1)}

    def ready(q, k):
        n3 = streams[q][2][2]
        k = min(k, n3 // 2)
        here = complete(q, k)
        for pair in range(n3 // 2):
            if pair not in done[q] and {2 * pair, 2 * pair + 1} <= here:
                done[q].add(pair)
                (take0, take1, take2)[q](pair)

    def steps_of(q):
        return streams[q][2][2] // 2 * parts_of(q)

    loaded = False
    for tau in range(items):
        for q in range(len(streams)):
            total = steps_of(q)
            stride = items // total
            if tau % stride == 0:
                i = tau // stride
                hop(q, i // parts_of(q) + 1, i % parts_of(q))
        if tau % 4 == 3 and tau + 1 < items:
            if not loaded:
                for load in loads:
                    load.wait()
                loaded = True
            for q in range(PIECES):
                sent = (tau // (items // steps_of(q)) + 1) // parts_of(q)
                ready(q, sent - 1)
    for q in range(len(streams)):
        n3 = streams[q][2][2]
        for i in range(parts_of(q)):
            for way in (0, 1):
                if n3 // 2 - way > 0:
                    landed(q, way, n3 // 2 - way, i)
    for slot in range(streams[META][2][2]):
        shared(META, slot)
    for q in (0, 2, 1):
        ready(q, streams[q][2][2])

    chips = nz * nx * ny
    expert = lax.axis_index("expert")
    lane = lax.broadcasted_iota(jnp.int32, (chips, LANES), 1)
    columns = []
    for c in range(2):
        meta = metas[c].reshape(chips, LANES)
        column = jnp.concatenate([
            jnp.sum(jnp.where(lane == j * 16 + expert, meta, 0.0), axis=1, keepdims=True)
            for j in range(2)
        ], axis=0)
        high = column.astype(BF16).astype(F32)
        middle = (column - high).astype(BF16).astype(F32)
        columns += [high, middle, column - high - middle]
    lane = lax.broadcasted_iota(jnp.int32, (2 * chips, LANES), 1)
    packed = jnp.zeros((2 * chips, LANES), F32)
    for i, column in enumerate(columns):
        packed = jnp.where(lane == i, column, packed)
    placed = jnp.dot(place_ref[...], packed.astype(BF16), preferred_element_type=F32)
    for c in range(2):
        total = placed[:, 3 * c:3 * c + 1] + placed[:, 3 * c + 1:3 * c + 2]
        total = total + placed[:, 3 * c + 2:3 * c + 3]
        weights[c] = jnp.broadcast_to(total, (2 * chips, LANES)).reshape(weights.shape[1:])

    span = 2 if nz >= 4 else 1
    chunks = nz // 2 // span

    def activate(i, _):
        where = (i // chunks, pl.ds(i % chunks * span, span))
        gate_pre, up_pre, down = rows_of(gate[where]), rows_of(up[where]), rows_of(grad[where])
        weight = rows_of(weights[where])[:, 0:1]
        down = down * weight
        sigma = jax.nn.sigmoid(gate_pre)
        active = gate_pre * sigma
        slope = sigma * (1.0 + gate_pre * (1.0 - sigma))
        shape = hidden[where].shape
        hidden[where] = (active * up_pre * weight).astype(BF16).reshape(shape)
        ggrad[where] = (down * up_pre * slope).astype(BF16).reshape(shape)
        ugrad[where] = (down * active).astype(BF16).reshape(shape)
        return 0

    lax.fori_loop(0, 2 * chunks, activate, 0)

    routes, sibs = (route0, route1, route2), (sib0, sib1, sib2)

    def expand(p, c):
        cols = slice(p * WIDE, (p + 1) * WIDE)

        def body(i, _):
            where = (c, pl.ds(i * span, span))
            term = jnp.dot(rows_of(ggrad[where]), wg[:, cols], preferred_element_type=F32)
            term = term + jnp.dot(rows_of(ugrad[where]), wu[:, cols], preferred_element_type=F32)
            term = term.astype(BF16)
            tile = lambda zi, yi, xi: ((zi * (ny // 2) + yi) * 2 + xi) * ROWS
            groups = []
            for zi in range(span):
                if p == 1:
                    for yq in range(ny // 4):
                        for xi in range(2):
                            starts = [tile(zi, 2 * yq, xi), tile(zi, 2 * yq + 1, xi)]
                            groups.append((zi, yq, xi, starts))
                else:
                    for yi in range(ny // 2):
                        starts = [tile(zi, yi, 0), tile(zi, yi, 1)]
                        groups.append((zi, yi, None, starts))
            for g in range(0, len(groups), 2):
                stacks = []
                for zi, b, xi, starts in groups[g:g + 2]:
                    stacks.append(jnp.concatenate([
                        term[start:start + ROWS, s * LANES:(s + 1) * LANES]
                        for s in range(SEGS) for start in starts
                    ], axis=0))
                moved = jnp.dot(
                    back_ref[p], jnp.concatenate(stacks, axis=1), preferred_element_type=F32
                ).astype(BF16)
                for n, (zi, b, xi, starts) in enumerate(groups[g:g + 2]):
                    value = moved[:, n * LANES:(n + 1) * LANES]
                    z = 2 * (i * span + zi)
                    if p == 0:
                        spot = (c, pl.ds(z, 2), slice(2 * b, 2 * b + 2))
                        value = value.reshape(2, 2, nx, ROWS, LANES)
                    elif p == 1:
                        spot = (c, slice(2 * xi, 2 * xi + 2), pl.ds(z, 2), slice(4 * b, 4 * b + 4))
                        value = value.reshape(2, 2, 4, ROWS, LANES)
                    else:
                        spot = (c, slice(2 * b, 2 * b + 2), slice(None), pl.ds(z, 2))
                        value = value.reshape(2, nx, 2, ROWS, LANES)
                    routes[p][spot] = value
            return 0

        lax.fori_loop(0, chunks, body, 0)

    for p in range(PIECES):
        expand(p, 1)
        push(routes[p].at[1], sibs[p], e_send.at[p], e_recv.at[p], other)
        expand(p, 0)

    lands, onces, nears = (land0, land1, land2), (once0, once1, once2), (near0, near1, near2)
    twices, lasts = (twice0, twice1, twice2), (last0, last1, last2)

    def total(dst, terms, count):
        def body(i, _):
            value = terms[0][i].astype(F32)
            for term in terms[1:]:
                value = value + term[i].astype(F32)
            dst[i] = value.astype(BF16)
            return 0

        lax.fori_loop(0, count, body, 0)

    def reduce_hop(p, t, h):
        order = ORDERS[p]
        n3, n2 = sizes[order[2]], sizes[order[1]]
        size = n2 // 4
        rows = pl.ds(h * size, size)
        for way in (0, 1):
            reach = n3 // 2 - way
            if t > reach:
                continue
            d = reach + 1 - t
            slot = n3 - d if way == 0 else d
            mine, theirs = routes[p].at[0, slot, rows], sibs[p].at[slot, rows]
            sem = (p, way, (t - 1) * 4 + h)
            if t == 1:
                total(theirs, [mine, theirs], size)
                src = theirs
            else:
                src = lands[p].at[way, t - 2, rows]
                before = (p, way, (t - 2) * 4 + h)
                arrived(src, a_send.at[before], a_recv.at[before])
                total(src, [src, mine, theirs], size)
            push(src, lands[p].at[way, t - 1, rows], a_send.at[sem], a_recv.at[sem],
                 grid.device(order[2], -1 if way == 0 else 1))

    chunk = 512

    def descend(i, _):
        cols = pl.ds(pl.multiple_of(i * chunk, chunk), chunk)
        lhs = hidden[...].reshape(4 * chips, hidden.shape[-1])
        rhs = xc[:, :, :, :, :, cols].reshape(4 * chips, chunk)
        dg_ref[:, cols] = lax.dot_general(
            lhs, rhs, (((0,), (0,)), ((), ())), preferred_element_type=F32
        ).astype(BF16)
        return 0

    for p in range(PIECES):
        arrived(sibs[p], e_send.at[p], e_recv.at[p])
    for tau in range(items):
        for p in range(PIECES):
            stride = items // (streams[p][2][2] // 2 * 4)
            if tau % stride == 0:
                i = tau // stride
                reduce_hop(p, i // 4 + 1, i % 4)
        if tau == 3:
            lax.fori_loop(0, 3, descend, 0)
        if tau == 7:
            lax.fori_loop(3, xc.shape[-1] // chunk, descend, 0)

    for p in range(PIECES):
        order = ORDERS[p]
        n1, n2, n3 = streams[p][2]
        terms = [routes[p].at[0, 0], sibs[p].at[0]]
        for way in (0, 1):
            reach = n3 // 2 - way
            if reach > 0:
                for h in range(4):
                    rows = pl.ds(h * (n2 // 4), n2 // 4)
                    sem = (p, way, (reach - 1) * 4 + h)
                    arrived(lands[p].at[way, reach - 1, rows], a_send.at[sem], a_recv.at[sem])
                terms.append(lands[p].at[way, reach - 1])
        total(onces[p], terms, n2)
        for r in nearest(n2):
            push(onces[p].at[r], nears[p].at[r - 1], b_send.at[p, r], b_recv.at[p, r],
                 grid.device(order[1], r))
    for p in range(PIECES):
        order = ORDERS[p]
        n1, n2, n3 = streams[p][2]
        value = onces[p][0].astype(F32)
        for r in nearest(n2):
            arrived(nears[p].at[r - 1], b_send.at[p, r], b_recv.at[p, r])
            value = value + nears[p][r - 1].astype(F32)
        twices[p][...] = value.astype(BF16)
        for r in nearest(n1):
            push(twices[p].at[r], lasts[p].at[r - 1], c_send.at[p, r], c_recv.at[p, r],
                 grid.device(order[0], r))
    for p in range(PIECES):
        n1 = streams[p][2][0]
        value = twices[p][0].astype(F32)
        for r in nearest(n1):
            arrived(lasts[p].at[r - 1], c_send.at[p, r], c_recv.at[p, r])
            value = value + lasts[p][r - 1].astype(F32)
        out_ref[p] = value.astype(BF16)

    for copy in pending:
        copy.wait_send()


def orders_of_rows(sizes):
    result = []
    for p, dims in enumerate((("z", "y", "x"), ("x", "z", "y"), ("y", "x", "z"))):
        long = "y" if p == 1 else "x"
        extent = {a: 4 if a == long else 2 for a in "xyz"}
        rows = []
        for s in range(SEGS):
            for tile in range(2):
                for j in range(2):
                    for z in range(2):
                        for y in range(2):
                            for x in range(2):
                                at = {"z": z, "y": y, "x": x}
                                at[long] += 2 * tile
                                device = 0
                                for a in dims:
                                    device = device * extent[a] + at[a]
                                rows.append((device * 2 + j) * SEGS + s)
        result.append(np.array(rows))
    return result


def order_of_weights(sizes):
    nz, nx, ny = sizes["z"], sizes["x"], sizes["y"]
    source = np.arange(2 * nx * nz * ny).reshape(2, nx // 2, 2, nz // 2, 2, ny // 2, 2)
    return source.transpose(3, 5, 1, 0, 4, 6, 2).reshape(-1)


def build(mesh, sizes):
    nz, nx, ny = sizes["z"], sizes["x"], sizes["y"]
    chips = nz * nx * ny
    experts = 16

    def on_device(tokens, cotangent, route_ids, gate_probs, w_gate, w_up, w_down):
        count, width = tokens.shape
        hid = w_gate.shape[2]
        matches = route_ids[:, :, None] == jnp.arange(experts, dtype=jnp.int32)[None, None, :]
        weights = jnp.sum(jnp.where(matches, gate_probs[:, :, None], 0.0), axis=1)
        meta = jnp.pad(weights.reshape(1, count * experts), ((0, 0), (0, LANES - count * experts)))

        def as_block(v):
            return v.reshape(count, PIECES, SEGS, LANES).transpose(1, 0, 2, 3).reshape(
                PIECES, ROWS, LANES
            )

        block = jnp.concatenate([as_block(tokens), as_block(cotangent)], axis=1)

        def one_hot(source):
            n = source.shape[0]
            return (jnp.asarray(source, jnp.int32)[:, None] == jnp.arange(n)[None, :]).astype(BF16)

        fores = [one_hot(rows) for rows in orders_of_rows(sizes)]
        fore = jnp.stack(fores)
        back = jnp.stack([f.T for f in fores])
        place = one_hot(order_of_weights(sizes))

        n = [tuple(sizes[a] for a in order) for order in ORDERS]
        vm = pl.BlockSpec(memory_space=pltpu.VMEM)
        hbm = pl.BlockSpec(memory_space=pl.ANY)
        dma = pltpu.SemaphoreType.DMA
        tiles = (2, nz // 2, ny // 2, nx // 2, ROWS)
        block_shape = (ROWS, LANES)
        most = max(nz, ny, nx)
        out, down = pl.pallas_call(
            functools.partial(kernel, sizes),
            out_shape=(
                jax.ShapeDtypeStruct((PIECES, ROWS, LANES), BF16),
                jax.ShapeDtypeStruct((hid, width), BF16),
            ),
            in_specs=[vm, vm, hbm, hbm, hbm, vm, vm, vm],
            out_specs=(vm, vm),
            scratch_shapes=[
                *[pltpu.VMEM((2, n3, n2, n1, 2 * ROWS, LANES), BF16) for n1, n2, n3 in n],
                pltpu.VMEM((2, n[1][2], n[1][1], n[1][0], 1, LANES), F32),
                pltpu.VMEM((*tiles, width), BF16),
                pltpu.VMEM((*tiles, width), BF16),
                pltpu.VMEM((hid, width), BF16),
                pltpu.VMEM((hid, width), BF16),
                pltpu.VMEM((hid, width), BF16),
                pltpu.VMEM((*tiles, LANES), F32),
                *[pltpu.VMEM((*tiles, hid), F32) for _ in range(3)],
                *[pltpu.VMEM((*tiles, hid), BF16) for _ in range(3)],
                *[pltpu.VMEM((2, n3, n2, n1, *block_shape), BF16) for n1, n2, n3 in n],
                *[pltpu.VMEM((n3, n2, n1, *block_shape), BF16) for n1, n2, n3 in n],
                *[pltpu.VMEM((2, n3 // 2, n2, n1, *block_shape), BF16) for n1, n2, n3 in n],
                *[pltpu.VMEM((n2, n1, *block_shape), BF16) for n1, n2, n3 in n],
                *[pltpu.VMEM((n2 - 1, n1, *block_shape), BF16) for n1, n2, n3 in n],
                *[pltpu.VMEM((n1, *block_shape), BF16) for n1, n2, n3 in n],
                *[pltpu.VMEM((n1 - 1, *block_shape), BF16) for n1, n2, n3 in n],
                dma((3,)),
                dma((4, most)), dma((4, most)),
                dma((4, most)), dma((4, most)),
                dma((4, 2, 2 * most)), dma((4, 2, 2 * most)),
                dma((4, most)), dma((4, most)),
                dma((3,)), dma((3,)),
                dma((3, 2, 2 * most)), dma((3, 2, 2 * most)),
                dma((3, most)), dma((3, most)),
                dma((3, most)), dma((3, most)),
            ],
            compiler_params=pltpu.CompilerParams(
                collective_id=0, has_side_effects=True, vmem_limit_bytes=62 * 1024 * 1024
            ),
            name="expert_backward",
        )(block, meta, w_gate[0].T, w_up[0].T, w_down[0], fore, back, place)
        grads = out.reshape(PIECES, count, SEGS, LANES).transpose(1, 0, 2, 3).reshape(count, width)
        return grads, down[None]

    both = P(("dp", "expert"), None)
    return jax.shard_map(
        on_device,
        mesh=mesh,
        in_specs=(both, both, both, both, P("expert", None, "dp"), P("expert", None, "dp"),
                  P("expert", "dp", None)),
        out_specs=(both, P("expert", "dp", None)),
        check_vma=False,
    )


def solution(mesh):
    across = 4
    sizes = {"z": mesh.shape["dp"] // across, "x": across, "y": mesh.shape["expert"] // 2}
    return build(mesh, sizes)
```

```python
import functools

import jax
import jax.numpy as jnp
from jax import lax
from jax.experimental import pallas as pl
from jax.experimental.pallas import tpu as pltpu
from jax.sharding import PartitionSpec as P

MESH = pl.DeviceIdType.MESH
F32 = jnp.float32
BF16 = jnp.bfloat16
PIECES = 3
ROWS = 16
LANES = 128
SEGS = 8
WIDE = SEGS * LANES
ORDERS = (("y", "x", "z"), ("y", "z", "x"), ("z", "x", "y"), ("y", "x", "z"))
META = 3


def nearest(n):
    return sorted(range(1, n), key=lambda r: min(r, n - r))


def flat(value):
    return value.reshape(-1, value.shape[-1])


class Grid:
    def __init__(self, sizes):
        self.n = sizes
        dp, ex = lax.axis_index("dp"), lax.axis_index("expert")
        self.at = {"z": dp // sizes["x"], "x": dp % sizes["x"], "y": ex // 2}
        self.core = ex % 2
        self.sign = 1 - 2 * self.core

    def device(self, axis=None, steps=0):
        at = dict(self.at)
        core = self.core
        if axis is None:
            core = 1 - core
        else:
            n = self.n[axis]
            at[axis] = (at[axis] + self.sign * steps + n) % n
        return (at["z"] * self.n["x"] + at["x"], at["y"] * 2 + core)


def one_hot(n, source):
    out = lax.broadcasted_iota(jnp.int32, (n, n), 0)
    return (lax.broadcasted_iota(jnp.int32, (n, n), 1) == source(out)).astype(F32).astype(BF16)


def kernel(
    sizes, tok_ref, cot_ref, ids_ref, probs_ref, wg_hbm, wu_hbm, wd_hbm, out_ref, dg_ref, *scratch
):
    scratch = list(scratch)

    def take(count):
        taken = tuple(scratch[:count])
        del scratch[:count]
        return taken

    first, tiles = take(3), take(3)
    (metas,) = take(1)
    wg, wu, wd, weights = take(4)
    gate, up, grad = take(3), take(3), take(3)
    hidden, ggrad, ugrad = take(3), take(3), take(3)
    routes, sibs, lands, onces, nears = take(3), take(3), take(3), take(3), take(3)
    twices, lasts = take(3), take(3)
    load_sem, g1_send, g1_recv, g2_send, g2_recv, g3_send, g3_recv = take(7)
    s_send, s_recv, e_send, e_recv, a_send, a_recv, b_send, b_recv, c_send, c_recv = take(10)

    grid = Grid(sizes)
    nz, nx, ny = sizes["z"], sizes["x"], sizes["y"]
    n1 = ny
    chips = nz * nx * ny
    other = grid.device()
    dims = [tuple(sizes[a] for a in order) for order in ORDERS]

    barrier = pltpu.get_barrier_semaphore()
    around = [other]
    for axis in ("x", "y", "z"):
        around += [grid.device(axis, r) for r in range(1, sizes[axis])]
    for device in around:
        pl.semaphore_signal(barrier, inc=1, device_id=device, device_id_type=MESH)

    loads = [
        pltpu.make_async_copy(src, dst, load_sem.at[i])
        for i, (src, dst) in enumerate(((wg_hbm, wg), (wu_hbm, wu), (wd_hbm, wd)))
    ]
    for load in loads:
        load.start()

    for half, ref in enumerate((tok_ref, cot_ref)):
        value = ref[...].astype(F32)
        for p in range(PIECES):
            rows = [
                value[:, p * WIDE + s * LANES:p * WIDE + (s + 1) * LANES] for s in range(SEGS)
            ]
            first[p][0, half * ROWS:(half + 1) * ROWS] = jnp.concatenate(rows, axis=0).astype(BF16)
    lane = lax.broadcasted_iota(jnp.int32, (1, LANES), 1)
    meta = jnp.zeros((1, LANES), F32)
    for j in range(ids_ref.shape[0]):
        for k in range(ids_ref.shape[1]):
            meta = meta + jnp.where(
                lane == ids_ref[j:j + 1, k:k + 1] + 16 * j, probs_ref[j:j + 1, k:k + 1], 0.0
            )
    metas[0, 0, 0, 0] = meta
    shift = n1.bit_length() - 1
    fore = one_hot(n1 * ROWS, lambda o: (o & (n1 - 1)) * ROWS + (o >> shift))
    back = one_hot(
        n1 * ROWS, lambda o: (o & (ROWS - 1)) * n1 + (o >> 4)
    )
    swap = one_hot(
        2 * n1 * n1,
        lambda o: (o & (n1 - 1)) * 2 * n1 + ((o >> shift) & 1) * n1 + (o >> (shift + 1)),
    )
    pl.semaphore_wait(barrier, len(around))

    pending = []

    def push(src, dst, ssem, rsem, device):
        copy = pltpu.make_async_remote_copy(
            src_ref=src, dst_ref=dst, send_sem=ssem, recv_sem=rsem,
            device_id=device, device_id_type=MESH,
        )
        copy.start()
        pending.append(copy)

    def arrived(dst, ssem, rsem):
        pltpu.make_async_remote_copy(
            src_ref=dst, dst_ref=dst, send_sem=ssem, recv_sem=rsem,
            device_id=other, device_id_type=MESH,
        ).wait_recv()

    held = [f for f in first] + [metas.at[0, 0, 0]]
    for q in range(4):
        for r in nearest(n1):
            push(held[q].at[0], held[q].at[n1 - r], g1_send.at[q, r], g1_recv.at[q, n1 - r],
                 grid.device(ORDERS[q][0], r))

    grids = list(tiles) + [metas]

    def send2(q, src, r):
        n2 = dims[q][1]
        dst = (src - r) % n2
        push(grids[q].at[0, 0, src], grids[q].at[0, 0, dst], g2_send.at[q, dst],
             g2_recv.at[q, dst], grid.device(ORDERS[q][1], r))

    def got2(q, r):
        arrived(grids[q].at[0, 0, r], g2_send.at[q, r], g2_recv.at[q, r])

    def one_step(q):
        return dims[q][1] <= 4

    for q in (1, 0, 2, META):
        for r in range(1, n1):
            arrived(held[q].at[r], g1_send.at[q, r], g1_recv.at[q, r])
        if q != META:
            both = jnp.concatenate([
                first[q][:, half * ROWS:(half + 1) * ROWS].reshape(n1 * ROWS, LANES)
                for half in range(2)
            ], axis=1)
            moved = jnp.dot(fore, both, preferred_element_type=F32).astype(BF16)
            for s in range(SEGS):
                cols = slice(s * LANES, (s + 1) * LANES)
                for half in range(2):
                    tiles[q][0, 0, 0, half, :, cols] = moved[
                        s * 2 * n1:(s + 1) * 2 * n1, half * LANES:(half + 1) * LANES
                    ]
        n2 = dims[q][1]
        for r in nearest(n2):
            if one_step(q) or min(r, n2 - r) <= 2:
                send2(q, 0, r)

    def turns_of(q):
        return (0,) if q == META else (0, *nearest(dims[q][1]))

    have = [{0} for _ in range(4)]

    def part(q, lead, h):
        return grids[q].at[lead] if q == META else grids[q].at[lead + (h,)]

    def share(q, slot):
        ref = grids[q]
        push(ref.at[0, slot], ref.at[1, slot], s_send.at[q, slot], s_recv.at[q, slot], other)

    def shared(q, slot):
        arrived(grids[q].at[1, slot], s_send.at[q, slot], s_recv.at[q, slot])

    def landed(q, way, k, i):
        n3 = dims[q][2]
        turns = turns_of(q)
        slot = n3 - k if way == 0 else k
        sem = (q, way, (k - 1) * len(turns) + i)
        arrived(part(q, (0, slot), turns[i]), g3_send.at[sem], g3_recv.at[sem])
        if i == len(turns) - 1:
            share(q, slot)

    def second(q, r):
        if r in have[q]:
            return
        n2 = dims[q][1]
        got2(q, r)
        have[q].add(r)
        if not one_step(q):
            if r == 2:
                send2(q, 2, -1)
                send2(q, 2, -2)
            if r == n2 - 2:
                send2(q, n2 - 2, 1)

    def hop(q, k, i):
        n2, n3 = dims[q][1:]
        turns = turns_of(q)
        h = turns[i]
        if k == 1:
            for r in range(n2) if q == META else (h,):
                second(q, r)
        for way in (0, 1):
            reach = n3 // 2 - way
            if 1 < k <= reach + 1:
                landed(q, way, k - 1, i)
            if k > reach:
                continue
            src = (n3 - (k - 1)) % n3 if way == 0 else k - 1
            dst = n3 - k if way == 0 else k
            sem = (q, way, (k - 1) * len(turns) + i)
            push(part(q, (0, src), h), part(q, (0, dst), h), g3_send.at[sem], g3_recv.at[sem],
                 grid.device(ORDERS[q][2], 1 if way == 0 else -1))
        if k == 1 and i == len(turns) - 1:
            share(q, 0)

    across = (((1,), (1,)), ((), ()))

    def multiply(p, at):
        cols = slice(p * WIDE, (p + 1) * WIDE)
        tok = flat(tiles[p][at + (slice(None), 0)])
        cot = flat(tiles[p][at + (slice(None), 1)])
        for acc, lhs, w in ((gate, tok, wg), (up, tok, wu), (grad, cot, wd)):
            result = lax.dot_general(lhs, w[:, cols], across, preferred_element_type=F32)
            acc[p][at] = result.reshape(acc[p].at[at].shape)

    done = set()

    def use(q, slot):
        done.add((q, slot))
        if q == 1:
            shared(1, slot)
            multiply(1, (slice(None), slice(slot, slot + 1)))
        elif (q, slot ^ 1) in done:
            low = slot & ~1
            shared(q, low)
            shared(q, low + 1)
            multiply(q, (slice(None), slice(low, low + 2)))

    hops = nz // 2
    items = 4 * hops
    for tau in range(items):
        for q in (1, 0, 2, META):
            turns = turns_of(q)
            total_items = dims[q][2] // 2 * len(turns)
            stride = items // total_items
            if tau % stride == 0:
                i = tau // stride
                hop(q, i // len(turns) + 1, i % len(turns))
        if tau == 3:
            for load in loads:
                load.wait()
        if tau % 4 == 3:
            k = tau // 4
            for q in (0, 2):
                use(q, (dims[q][2] - k) % dims[q][2])
                if 0 < k <= dims[q][2] // 2 - 1:
                    use(q, k)
            if tau == items // 2 - 1:
                use(1, 0)

    def weigh():
        for slot in range(nz):
            shared(META, slot)
        expert = lax.axis_index("expert")
        lane = lax.broadcasted_iota(jnp.int32, (chips, LANES), 1)
        for c in range(2):
            meta = metas[c].reshape(chips, LANES)
            halves = [
                jnp.broadcast_to(
                    jnp.sum(jnp.where(lane == j * 16 + expert, meta, 0.0), axis=1, keepdims=True),
                    (chips, LANES),
                )
                for j in range(2)
            ]
            for j in range(2):
                weights[c, :, :, j] = halves[j].reshape(nz, nx, ny, LANES)

    for slot in range(1, nx):
        if slot != nx // 2:
            use(1, slot)
    landed(META, 0, nz // 2, 0)
    for q in (0, 2):
        for i in range(len(turns_of(q))):
            landed(q, 0, dims[q][2] // 2, i)
    weigh()
    for q in (0, 2):
        use(q, dims[q][2] // 2)
    for i in range(nz):
        landed(1, 0, nx // 2, i)
    use(1, nx // 2)

    def activate(i, _):
        c, x = i // nx, i % nx
        late = []
        for acc in (gate, up, grad):
            value = flat(acc[2][c, :, x])
            high = value.astype(BF16)
            late += [high, (value - high.astype(F32)).astype(BF16)]
        turned = [jnp.dot(swap, v, preferred_element_type=F32) for v in late]
        gate_pre, up_pre, down = [
            flat(acc[0][c, :, x]) + flat(acc[1][c, x]) + turned[2 * n] + turned[2 * n + 1]
            for n, acc in enumerate((gate, up, grad))
        ]
        weight = flat(weights[c, :, x])[:, 0:1]
        down = down * weight
        sigma = jax.nn.sigmoid(gate_pre)
        active = gate_pre * sigma
        slope = sigma * (1.0 + gate_pre * (1.0 - sigma))
        for ref, value in (
            (hidden, active * up_pre * weight), (ggrad, down * up_pre * slope), (ugrad, down * active)
        ):
            value = value.astype(BF16)
            shape = ref[1].shape[2:]
            ref[0][c, :, x] = value.reshape(shape)
            ref[1][c, x] = value.reshape(shape)
            value = jnp.dot(swap, value, preferred_element_type=F32).astype(BF16)
            ref[2][c, :, x] = value.reshape(shape)
        return 0

    lax.fori_loop(0, 2 * nx, activate, 0)

    def expand(p, c, half):
        cols = slice(p * WIDE, (p + 1) * WIDE)
        n3 = dims[p][2]
        rows = (c, slice(half * n3 // 2, (half + 1) * n3 // 2))
        term = jnp.dot(flat(ggrad[p][rows]), wg[:, cols], preferred_element_type=F32)
        term = term + jnp.dot(flat(ugrad[p][rows]), wu[:, cols], preferred_element_type=F32)
        routes[p][rows] = term.astype(BF16).reshape(routes[p].at[rows].shape)

    def total(dst, terms, index):
        value = terms[0][index].astype(F32)
        for term in terms[1:]:
            value = value + term[index].astype(F32)
        dst[index] = value.astype(BF16)

    def reduce_hop(p, t, h):
        n2, n3 = dims[p][1:]
        for way in (0, 1):
            reach = n3 // 2 - way
            if t > reach:
                continue
            d = reach + 1 - t
            slot = n3 - d if way == 0 else d
            mine, theirs = routes[p].at[0, slot], sibs[p].at[slot]
            sem = (p, way, (t - 1) * n2 + h)
            if t == 1:
                total(theirs, [mine, theirs], h)
                src = theirs.at[h]
            else:
                land = lands[p].at[way, t - 2]
                src = land.at[h]
                before = (p, way, (t - 2) * n2 + h)
                arrived(src, a_send.at[before], a_recv.at[before])
                total(land, [land, mine, theirs], h)
            push(src, lands[p].at[way, t - 1, h], a_send.at[sem], a_recv.at[sem],
                 grid.device(ORDERS[p][2], -1 if way == 0 else 1))

    chunk = WIDE // 2

    def descend(p, half):
        cols = slice(p * WIDE + half * chunk, p * WIDE + (half + 1) * chunk)
        rhs = tiles[p][:, :, :, 1, :, half * chunk:(half + 1) * chunk]
        dg_ref[:, cols] = lax.dot_general(
            flat(hidden[p][...]), flat(rhs), (((0,), (0,)), ((), ())), preferred_element_type=F32
        ).astype(BF16)

    order = (0, 2, 1)
    for p in order:
        n3 = dims[p][2]
        for half in (1, 0):
            expand(p, 1, half)
            some = pl.ds(half * n3 // 2, n3 // 2)
            push(routes[p].at[1, some], sibs[p].at[some], e_send.at[p, half], e_recv.at[p, half],
                 other)
    for p in order:
        n3 = dims[p][2]
        for half in (1, 0):
            expand(p, 0, half)
            some = pl.ds(half * n3 // 2, n3 // 2)
            arrived(sibs[p].at[some], e_send.at[p, half], e_recv.at[p, half])
        for h in range(dims[p][1]):
            reduce_hop(p, 1, h)
    for tau in range(4, items):
        for p in order:
            n2, n3 = dims[p][1:]
            stride = items // (n3 // 2 * n2)
            if tau % stride == 0 and tau // stride >= n2:
                i = tau // stride
                reduce_hop(p, i // n2 + 1, i % n2)
        if tau % 4 == 3:
            k = tau // 4 - 1
            if k < 3:
                descend(k, 0)
                descend(k, 1)

    for p in order:
        n2, n3 = dims[p][1:]
        for h in (*nearest(n2), 0):
            terms = [routes[p].at[0, 0], sibs[p].at[0]]
            for way in (0, 1):
                reach = n3 // 2 - way
                if reach > 0:
                    sem = (p, way, (reach - 1) * n2 + h)
                    land = lands[p].at[way, reach - 1]
                    arrived(land.at[h], a_send.at[sem], a_recv.at[sem])
                    terms.append(land)
            total(onces[p], terms, h)
            if h > 0:
                push(onces[p].at[h], nears[p].at[h - 1], b_send.at[p, h], b_recv.at[p, h],
                     grid.device(ORDERS[p][1], h))
    for p in order:
        n2 = dims[p][1]
        value = onces[p][0].astype(F32)
        for r in nearest(n2):
            arrived(nears[p].at[r - 1], b_send.at[p, r], b_recv.at[p, r])
            value = value + nears[p][r - 1].astype(F32)
        value = value.astype(BF16)
        stack = jnp.concatenate(
            [value[:, s * LANES:(s + 1) * LANES] for s in range(SEGS)], axis=0
        )
        moved = jnp.dot(back, stack, preferred_element_type=F32).astype(BF16)
        twices[p][...] = moved.reshape(n1, ROWS, LANES)
        for r in nearest(n1):
            push(twices[p].at[r], lasts[p].at[r - 1], c_send.at[p, r], c_recv.at[p, r],
                 grid.device(ORDERS[p][0], r))
    for p in order:
        value = twices[p][0].astype(F32)
        for r in nearest(n1):
            arrived(lasts[p].at[r - 1], c_send.at[p, r], c_recv.at[p, r])
            value = value + lasts[p][r - 1].astype(F32)
        count = out_ref.shape[0]
        for s in range(SEGS):
            cols = slice(p * WIDE + s * LANES, p * WIDE + (s + 1) * LANES)
            out_ref[:, cols] = value[s * count:(s + 1) * count].astype(BF16)

    for copy in pending:
        copy.wait_send()


def build(mesh, sizes):
    nz, nx, ny = sizes["z"], sizes["x"], sizes["y"]
    assert ny == nz

    def on_device(tokens, cotangent, route_ids, gate_probs, w_gate, w_up, w_down):
        count, width = tokens.shape
        hid = w_gate.shape[2]
        n = [tuple(sizes[a] for a in order) for order in ORDERS]
        vm = pl.BlockSpec(memory_space=pltpu.VMEM)
        hbm = pl.BlockSpec(memory_space=pl.ANY)
        dma = pltpu.SemaphoreType.DMA
        rows = 2 * ny

        def each(shape_of, dtype=BF16):
            return [pltpu.VMEM(shape_of(*n[p]), dtype) for p in range(PIECES)]

        def sums(dtype):
            return each(lambda n1, n2, n3: (2, n3, n2, rows, hid), dtype)

        most = max(nz, ny, nx)
        out, down = pl.pallas_call(
            functools.partial(kernel, sizes),
            out_shape=(
                jax.ShapeDtypeStruct((count, width), BF16),
                jax.ShapeDtypeStruct((hid, width), BF16),
            ),
            in_specs=[vm, vm, vm, vm, hbm, hbm, hbm],
            out_specs=(vm, vm),
            scratch_shapes=[
                *each(lambda n1, n2, n3: (n1, 2 * ROWS, LANES)),
                *each(lambda n1, n2, n3: (2, n3, n2, 2, rows, WIDE)),
                pltpu.VMEM((2, nz, nx, ny, 1, LANES), F32),
                *[pltpu.VMEM((hid, width), BF16) for _ in range(3)],
                pltpu.VMEM((2, nz, nx, 2, ny, LANES), F32),
                *sums(F32), *sums(F32), *sums(F32),
                *sums(BF16), *sums(BF16), *sums(BF16),
                *each(lambda n1, n2, n3: (2, n3, n2, rows, WIDE)),
                *each(lambda n1, n2, n3: (n3, n2, rows, WIDE)),
                *each(lambda n1, n2, n3: (2, n3 // 2, n2, rows, WIDE)),
                *each(lambda n1, n2, n3: (n2, rows, WIDE)),
                *each(lambda n1, n2, n3: (n2 - 1, rows, WIDE)),
                *each(lambda n1, n2, n3: (n1, ROWS, LANES)),
                *each(lambda n1, n2, n3: (n1 - 1, ROWS, LANES)),
                dma((3,)),
                dma((4, most)), dma((4, most)),
                dma((4, most)), dma((4, most)),
                dma((4, 2, 2 * most)), dma((4, 2, 2 * most)),
                dma((4, most)), dma((4, most)),
                dma((3, 2)), dma((3, 2)),
                dma((3, 2, 2 * most)), dma((3, 2, 2 * most)),
                dma((3, most)), dma((3, most)),
                dma((3, most)), dma((3, most)),
            ],
            compiler_params=pltpu.CompilerParams(
                collective_id=0, has_side_effects=True, vmem_limit_bytes=62 * 1024 * 1024
            ),
            name="expert_backward",
        )(tokens, cotangent, route_ids, gate_probs, w_gate[0].T, w_up[0].T, w_down[0])
        return out, down[None]

    both = P(("dp", "expert"), None)
    return jax.shard_map(
        on_device,
        mesh=mesh,
        in_specs=(both, both, both, both, P("expert", None, "dp"), P("expert", None, "dp"),
                  P("expert", "dp", None)),
        out_specs=(both, P("expert", "dp", None)),
        check_vma=False,
    )


def solution(mesh):
    across = 4
    sizes = {"z": mesh.shape["dp"] // across, "x": across, "y": mesh.shape["expert"] // 2}
    return build(mesh, sizes)
```

```python
import functools

import jax
import jax.numpy as jnp
from jax import lax
from jax.experimental import pallas as pl
from jax.experimental.pallas import tpu as pltpu
from jax.sharding import PartitionSpec as P

MESH = pl.DeviceIdType.MESH
F32 = jnp.float32
BF16 = jnp.bfloat16
PIECES = 3
ROWS = 16
LANES = 128
SEGS = 8
WIDE = SEGS * LANES
ORDERS = (("y", "x", "z"), ("y", "z", "x"), ("z", "x", "y"), ("y", "x", "z"))
META = 3


def nearest(n):
    return sorted(range(1, n), key=lambda r: min(r, n - r))


def flat(value):
    return value.reshape(-1, value.shape[-1])


class Grid:
    def __init__(self, sizes):
        self.n = sizes
        dp, ex = lax.axis_index("dp"), lax.axis_index("expert")
        self.at = {"z": dp // sizes["x"], "x": dp % sizes["x"], "y": ex // 2}
        self.core = ex % 2
        self.sign = 1 - 2 * self.core

    def device(self, axis=None, steps=0):
        at = dict(self.at)
        core = self.core
        if axis is None:
            core = 1 - core
        else:
            n = self.n[axis]
            at[axis] = (at[axis] + self.sign * steps + n) % n
        return (at["z"] * self.n["x"] + at["x"], at["y"] * 2 + core)


def one_hot(n, source):
    out = lax.broadcasted_iota(jnp.int32, (n, n), 0)
    return (lax.broadcasted_iota(jnp.int32, (n, n), 1) == source(out)).astype(F32).astype(BF16)


def kernel(
    sizes, tok_ref, cot_ref, ids_ref, probs_ref, wg_hbm, wu_hbm, wd_hbm, out_ref, dg_ref, *scratch
):
    scratch = list(scratch)

    def take(count):
        taken = tuple(scratch[:count])
        del scratch[:count]
        return taken

    first, tiles = take(3), take(3)
    (metas,) = take(1)
    wg, wu, wd, weights = take(4)
    gate, up, grad = take(3), take(3), take(3)
    hidden, ggrad, ugrad = take(3), take(3), take(3)
    routes, sibs, lands, onces, nears = take(3), take(3), take(3), take(3), take(3)
    twices, lasts = take(3), take(3)
    (dg,) = take(1)
    opposite = take(3)
    load_sem, sent, g1_recv, g2_recv, g3_recv, s_recv = take(6)
    e_recv, o_recv, a_recv, b_recv, c_recv = take(5)

    grid = Grid(sizes)
    nz, nx, ny = sizes["z"], sizes["x"], sizes["y"]
    n1 = ny
    chips = nz * nx * ny
    other = grid.device()
    dims = [tuple(sizes[a] for a in order) for order in ORDERS]

    barrier = pltpu.get_barrier_semaphore()
    around = [other]
    for axis in ("x", "y", "z"):
        around += [grid.device(axis, r) for r in range(1, sizes[axis])]
    for device in around:
        pl.semaphore_signal(barrier, inc=1, device_id=device, device_id_type=MESH)

    loads = [
        pltpu.make_async_copy(src, dst, load_sem.at[i])
        for i, (src, dst) in enumerate(((wg_hbm, wg), (wu_hbm, wu), (wd_hbm, wd)))
    ]
    for load in loads:
        load.start()

    for half, ref in enumerate((tok_ref, cot_ref)):
        value = ref[...].astype(F32)
        for p in range(PIECES):
            rows = [
                value[:, p * WIDE + s * LANES:p * WIDE + (s + 1) * LANES] for s in range(SEGS)
            ]
            first[p][0, half * ROWS:(half + 1) * ROWS] = jnp.concatenate(rows, axis=0).astype(BF16)
    lane = lax.broadcasted_iota(jnp.int32, (1, LANES), 1)
    meta = jnp.zeros((1, LANES), F32)
    for j in range(ids_ref.shape[0]):
        for k in range(ids_ref.shape[1]):
            meta = meta + jnp.where(
                lane == ids_ref[j:j + 1, k:k + 1] + 16 * j, probs_ref[j:j + 1, k:k + 1], 0.0
            )
    metas[0, 0, 0, 0] = meta
    shift = n1.bit_length() - 1
    fore = one_hot(n1 * ROWS, lambda o: (o & (n1 - 1)) * ROWS + (o >> shift))
    back = one_hot(
        n1 * ROWS, lambda o: (o & (ROWS - 1)) * n1 + (o >> 4)
    )
    swap = one_hot(
        2 * n1 * n1,
        lambda o: (o & (n1 - 1)) * 2 * n1 + ((o >> shift) & 1) * n1 + (o >> (shift + 1)),
    )
    pl.semaphore_wait(barrier, len(around))

    def copy_of(src, dst, ssem, rsem, device):
        return pltpu.make_async_remote_copy(
            src_ref=src, dst_ref=dst, send_sem=ssem, recv_sem=rsem,
            device_id=device, device_id_type=MESH,
        )

    def push(src, dst, kind, q, rsem, device):
        copy_of(src, dst, sent.at[kind, q], rsem, device).start()

    def arrived(dst, rsem):
        copy_of(dst, dst, sent.at[0, 0], rsem, other).wait_recv()

    def drain(ref, kind, q):
        copy_of(ref, ref, sent.at[kind, q], g1_recv.at[0], other).wait_send()

    held = [f for f in first] + [metas.at[0, 0, 0]]
    for q in range(4):
        for r in nearest(n1):
            push(held[q].at[0], held[q].at[n1 - r], 0, q, g1_recv.at[q],
                 grid.device(ORDERS[q][0], r))

    grids = list(tiles) + [metas]

    def send2(q, src, r):
        n2 = dims[q][1]
        dst = (src - r) % n2
        push(grids[q].at[0, 0, src], grids[q].at[0, 0, dst], 1, q, g2_recv.at[q, dst],
             grid.device(ORDERS[q][1], r))

    def got2(q, r):
        arrived(grids[q].at[0, 0, r], g2_recv.at[q, r])

    def one_step(q):
        return dims[q][1] <= 4

    for q in (1, 0, 2, META):
        arrived(held[q].at[pl.ds(1, n1 - 1)], g1_recv.at[q])
        if q != META:
            both = jnp.concatenate([
                first[q][:, half * ROWS:(half + 1) * ROWS].reshape(n1 * ROWS, LANES)
                for half in range(2)
            ], axis=1)
            moved = jnp.dot(fore, both, preferred_element_type=F32).astype(BF16)
            for s in range(SEGS):
                cols = slice(s * LANES, (s + 1) * LANES)
                for half in range(2):
                    tiles[q][0, 0, 0, half, :, cols] = moved[
                        s * 2 * n1:(s + 1) * 2 * n1, half * LANES:(half + 1) * LANES
                    ]
        n2 = dims[q][1]
        for r in nearest(n2):
            if one_step(q) or min(r, n2 - r) <= 2:
                send2(q, 0, r)

    def turns_of(q):
        return {0: (0, 1), 1: (0, 3, 1, 2), 2: (0, 1), META: (0,)}[q]

    have = [{0} for _ in range(4)]

    def part(q, lead, h):
        return grids[q].at[lead] if q == META else grids[q].at[lead + (pl.ds(2 * h, 2),)]

    def share(q, slot):
        ref = grids[q]
        if q != META:
            push(ref.at[0, slot], ref.at[1, slot], 3, q, s_recv.at[q, slot], other)

    def shared(q, slot):
        arrived(grids[q].at[1, slot], s_recv.at[q, slot])

    def landed(q, way, k, i):
        n3 = dims[q][2]
        turns = turns_of(q)
        slot = n3 - k if way == 0 else k
        sem = (q, way, (k - 1) * len(turns) + i)
        arrived(part(q, (0, slot), turns[i]), g3_recv.at[sem])
        if i == len(turns) - 1:
            share(q, slot)

    def second(q, r):
        if r in have[q]:
            return
        n2 = dims[q][1]
        got2(q, r)
        have[q].add(r)
        if not one_step(q):
            if r == 2:
                send2(q, 2, -1)
                send2(q, 2, -2)
            if r == n2 - 2:
                send2(q, n2 - 2, 1)

    def hop(q, k, i):
        n2, n3 = dims[q][1:]
        turns = turns_of(q)
        h = turns[i]
        if k == 1:
            for r in range(n2) if q == META else (2 * h, 2 * h + 1):
                second(q, r)
        for way in (0, 1):
            reach = n3 // 2 - way
            if 1 < k <= reach + 1:
                landed(q, way, k - 1, i)
            if k > reach:
                continue
            src = (n3 - (k - 1)) % n3 if way == 0 else k - 1
            dst = n3 - k if way == 0 else k
            sem = (q, way, (k - 1) * len(turns) + i)
            push(part(q, (0, src), h), part(q, (0, dst), h), 2, q, g3_recv.at[sem],
                 grid.device(ORDERS[q][2], 1 if way == 0 else -1))
        if k == 1 and i == len(turns) - 1:
            share(q, 0)

    across = (((1,), (1,)), ((), ()))

    def multiply(p, at):
        cols = slice(p * WIDE, (p + 1) * WIDE)
        tok = flat(tiles[p][at + (slice(None), 0)])
        cot = flat(tiles[p][at + (slice(None), 1)])
        for acc, lhs, w in ((gate, tok, wg), (up, tok, wu), (grad, cot, wd)):
            result = lax.dot_general(lhs, w[:, cols], across, preferred_element_type=F32)
            acc[p][at] = result.reshape(acc[p].at[at].shape)

    done = set()

    def use(q, slot):
        done.add((q, slot))
        if q == 1:
            shared(1, slot)
            multiply(1, (slice(None), slice(slot, slot + 1)))
        elif (q, slot ^ 1) in done:
            low = slot & ~1
            shared(q, low)
            shared(q, low + 1)
            multiply(q, (slice(None), slice(low, low + 2)))

    items = 8
    starts = ((0, 1, 3, 3), (2, 4, 6, 7))
    for tau in range(items):
        for q in (0, 2):
            hop(q, tau // 2 + 1, tau % 2)
        for k in range(2):
            for i in range(4):
                if starts[k][i] == tau:
                    hop(1, k + 1, i)
        if tau % 2 == 0:
            hop(META, tau // 2 + 1, 0)
        if tau == 1:
            for load in loads:
                load.wait()
        if tau % 2 == 1:
            k = tau // 2
            for q in (0, 2):
                use(q, (dims[q][2] - k) % dims[q][2])
                if 0 < k <= dims[q][2] // 2 - 1:
                    use(q, k)
        if tau == 6:
            use(1, 0)

    def weigh():
        arrived(metas.at[1], s_recv.at[META, 0])
        expert = lax.axis_index("expert")
        lane = lax.broadcasted_iota(jnp.int32, (chips, LANES), 1)
        for c in range(2):
            meta = metas[c].reshape(chips, LANES)
            halves = [
                jnp.broadcast_to(
                    jnp.sum(jnp.where(lane == j * 16 + expert, meta, 0.0), axis=1, keepdims=True),
                    (chips, LANES),
                )
                for j in range(2)
            ]
            for j in range(2):
                weights[c, :, :, j] = halves[j].reshape(nz, nx, ny, LANES)

    for slot in range(1, nx):
        if slot != nx // 2:
            use(1, slot)
    landed(META, 0, nz // 2, 0)
    push(metas.at[0], metas.at[1], 3, META, s_recv.at[META, 0], other)
    weigh()
    for q in (0, 2):
        for i in range(len(turns_of(q))):
            landed(q, 0, dims[q][2] // 2, i)
    for q in (0, 2):
        use(q, dims[q][2] // 2)
    for i in range(len(turns_of(1))):
        landed(1, 0, nx // 2, i)
    use(1, nx // 2)

    def activate(i, _):
        c, x = i // nx, i % nx
        late = []
        for acc in (gate, up, grad):
            value = flat(acc[2][c, :, x])
            high = value.astype(BF16)
            late += [high, (value - high.astype(F32)).astype(BF16)]
        turned = [jnp.dot(swap, v, preferred_element_type=F32) for v in late]
        gate_pre, up_pre, down = [
            flat(acc[0][c, :, x]) + flat(acc[1][c, x]) + turned[2 * n] + turned[2 * n + 1]
            for n, acc in enumerate((gate, up, grad))
        ]
        weight = flat(weights[c, :, x])[:, 0:1]
        down = down * weight
        sigma = jax.nn.sigmoid(gate_pre)
        active = gate_pre * sigma
        slope = sigma * (1.0 + gate_pre * (1.0 - sigma))
        for ref, value in (
            (hidden, active * up_pre * weight), (ggrad, down * up_pre * slope), (ugrad, down * active)
        ):
            value = value.astype(BF16)
            shape = ref[1].shape[2:]
            ref[0][c, :, x] = value.reshape(shape)
            ref[1][c, x] = value.reshape(shape)
            value = jnp.dot(swap, value, preferred_element_type=F32).astype(BF16)
            ref[2][c, :, x] = value.reshape(shape)
        return 0

    lax.fori_loop(0, 2 * nx, activate, 0)

    def expand(p, c, half):
        cols = slice(p * WIDE, (p + 1) * WIDE)
        n3 = dims[p][2]
        rows = (c, slice(half * n3 // 2, (half + 1) * n3 // 2))
        term = jnp.dot(flat(ggrad[p][rows]), wg[:, cols], preferred_element_type=F32)
        term = term + jnp.dot(flat(ugrad[p][rows]), wu[:, cols], preferred_element_type=F32)
        routes[p][rows] = term.astype(BF16).reshape(routes[p].at[rows].shape)

    def total(dst, terms, indices):
        for index in indices:
            value = terms[0][index].astype(F32)
            for term in terms[1:]:
                value = value + term[index].astype(F32)
            dst[index] = value.astype(BF16)

    def reach_of(p, way):
        n3 = dims[p][2]
        return 3 if n3 == 8 else n3 // 2 - way

    def reduce_hop(p, t, h):
        n2, n3 = dims[p][1:]
        rows, some = (2 * h, 2 * h + 1), pl.ds(2 * h, 2)
        parts = n2 // 2
        if t == 1 and n3 == 8:
            theirs = sibs[p].at[4]
            total(theirs, [routes[p].at[0, 4], theirs], rows)
            push(theirs.at[some], opposite[p].at[some], 5, p, o_recv.at[p, h],
                 grid.device(ORDERS[p][2], -2))
        for way in (0, 1):
            reach = reach_of(p, way)
            if t > reach:
                continue
            d = reach + 1 - t
            slot = n3 - d if way == 0 else d
            mine, theirs = routes[p].at[0, slot], sibs[p].at[slot]
            sem = (p, way, (t - 1) * parts + h)
            if t == 1:
                total(theirs, [mine, theirs], rows)
                src = theirs.at[some]
            else:
                land = lands[p].at[way, t - 2]
                src = land.at[some]
                terms = [land, mine, theirs]
                if n3 == 8 and t == 2 and way == 0:
                    arrived(opposite[p].at[some], o_recv.at[p, h])
                    terms.append(opposite[p])
                arrived(src, a_recv.at[p, way, (t - 2) * parts + h])
                total(land, terms, rows)
            push(src, lands[p].at[way, t - 1, some], 5, p, a_recv.at[sem],
                 grid.device(ORDERS[p][2], -1 if way == 0 else 1))

    chunk = WIDE // 2

    def descend(p, half):
        cols = slice(p * WIDE + half * chunk, p * WIDE + (half + 1) * chunk)
        rhs = tiles[p][:, :, :, 1, :, half * chunk:(half + 1) * chunk]
        dg[:, cols] = lax.dot_general(
            flat(hidden[p][...]), flat(rhs), (((0,), (0,)), ((), ())), preferred_element_type=F32
        ).astype(BF16)

    def hand_over(p):
        n3 = dims[p][2]
        for half in (1, 0):
            expand(p, 1, half)
            some = pl.ds(half * n3 // 2, n3 // 2)
            push(routes[p].at[1, some], sibs[p].at[some], 4, p, e_recv.at[p, half], other)

    def set_out(p):
        n3 = dims[p][2]
        for half in (1, 0):
            expand(p, 0, half)
        for half in (1, 0):
            some = pl.ds(half * n3 // 2, n3 // 2)
            arrived(sibs[p].at[some], e_recv.at[p, half])
        for h in range(dims[p][1] // 2):
            reduce_hop(p, 1, h)

    def settle(p, h):
        n2, n3 = dims[p][1:]
        rows, some = (2 * h, 2 * h + 1), pl.ds(2 * h, 2)
        terms = [routes[p].at[0, 0], sibs[p].at[0]]
        for way in (0, 1):
            reach = reach_of(p, way)
            land = lands[p].at[way, reach - 1]
            arrived(land.at[some], a_recv.at[p, way, (reach - 1) * (n2 // 2) + h])
            terms.append(land)
        total(onces[p], terms, rows)
        for r in rows:
            if r > 0:
                push(onces[p].at[r], nears[p].at[r - 1], 6, p, b_recv.at[p],
                     grid.device(ORDERS[p][1], r))

    hand_over(0)
    hand_over(2)
    set_out(0)
    hand_over(1)
    set_out(2)
    set_out(1)
    for tau in range(2, 6):
        for p in (0, 2):
            reduce_hop(p, tau // 2 + 1, tau % 2)
        if tau == 3:
            for h in (0, 1, 2, 3):
                reduce_hop(1, 2, h)
            for p in range(PIECES):
                descend(p, 0)
        if tau == 5:
            for h in (0, 1, 2, 3):
                settle(1, h)
    for p in range(PIECES):
        descend(p, 1)
    store = pltpu.make_async_copy(dg, dg_ref, load_sem.at[0])
    store.start()
    for h in (0, 1):
        for p in (0, 2):
            settle(p, h)

    order = (0, 2, 1)
    for p in order:
        n2 = dims[p][1]
        value = onces[p][0].astype(F32)
        arrived(nears[p], b_recv.at[p])
        for r in nearest(n2):
            value = value + nears[p][r - 1].astype(F32)
        value = value.astype(BF16)
        stack = jnp.concatenate(
            [value[:, s * LANES:(s + 1) * LANES] for s in range(SEGS)], axis=0
        )
        moved = jnp.dot(back, stack, preferred_element_type=F32).astype(BF16)
        twices[p][...] = moved.reshape(n1, ROWS, LANES)
        for r in nearest(n1):
            push(twices[p].at[r], lasts[p].at[r - 1], 7, p, c_recv.at[p],
                 grid.device(ORDERS[p][0], r))
    for p in order:
        value = twices[p][0].astype(F32)
        arrived(lasts[p], c_recv.at[p])
        for r in nearest(n1):
            value = value + lasts[p][r - 1].astype(F32)
        count = out_ref.shape[0]
        for s in range(SEGS):
            cols = slice(p * WIDE + s * LANES, p * WIDE + (s + 1) * LANES)
            out_ref[:, cols] = value[s * count:(s + 1) * count].astype(BF16)

    for q in range(4):
        n2, n3 = dims[q][1:]
        drain(held[q].at[pl.ds(0, n1 - 1)], 0, q)
        drain(grids[q].at[0, 0, pl.ds(0, n2 - 1)], 1, q)
        drain(grids[q].at[0, pl.ds(0, n3 - 1)], 2, q)
        drain(grids[q].at[0], 3, q)
    for p in range(PIECES):
        n2, n3 = dims[p][1:]
        drain(routes[p].at[1], 4, p)
        drain(sibs[p].at[pl.ds(0, n3 - 1)], 5, p)
        drain(onces[p].at[pl.ds(0, n2 - 1)], 6, p)
        drain(twices[p].at[pl.ds(0, n1 - 1)], 7, p)
    store.wait()


def build(mesh, sizes):
    nz, nx, ny = sizes["z"], sizes["x"], sizes["y"]
    assert ny == nz

    def on_device(tokens, cotangent, route_ids, gate_probs, w_gate, w_up, w_down):
        count, width = tokens.shape
        hid = w_gate.shape[2]
        n = [tuple(sizes[a] for a in order) for order in ORDERS]
        vm = pl.BlockSpec(memory_space=pltpu.VMEM)
        hbm = pl.BlockSpec(memory_space=pl.ANY)
        dma = pltpu.SemaphoreType.DMA
        rows = 2 * ny

        def each(shape_of, dtype=BF16):
            return [pltpu.VMEM(shape_of(*n[p]), dtype) for p in range(PIECES)]

        def sums(dtype):
            return each(lambda n1, n2, n3: (2, n3, n2, rows, hid), dtype)

        most = max(nz, ny, nx)
        out, down = pl.pallas_call(
            functools.partial(kernel, sizes),
            out_shape=(
                jax.ShapeDtypeStruct((count, width), BF16),
                jax.ShapeDtypeStruct((hid, width), BF16),
            ),
            in_specs=[vm, vm, vm, vm, hbm, hbm, hbm],
            out_specs=(vm, hbm),
            scratch_shapes=[
                *each(lambda n1, n2, n3: (n1, 2 * ROWS, LANES)),
                *each(lambda n1, n2, n3: (2, n3, n2, 2, rows, WIDE)),
                pltpu.VMEM((2, nz, nx, ny, 1, LANES), F32),
                *[pltpu.VMEM((hid, width), BF16) for _ in range(3)],
                pltpu.VMEM((2, nz, nx, 2, ny, LANES), F32),
                *sums(F32), *sums(F32), *sums(F32),
                *sums(BF16), *sums(BF16), *sums(BF16),
                *each(lambda n1, n2, n3: (2, n3, n2, rows, WIDE)),
                *each(lambda n1, n2, n3: (n3, n2, rows, WIDE)),
                *each(lambda n1, n2, n3: (2, n3 // 2, n2, rows, WIDE)),
                *each(lambda n1, n2, n3: (n2, rows, WIDE)),
                *each(lambda n1, n2, n3: (n2 - 1, rows, WIDE)),
                *each(lambda n1, n2, n3: (n1, ROWS, LANES)),
                *each(lambda n1, n2, n3: (n1 - 1, ROWS, LANES)),
                pltpu.VMEM((hid, width), BF16),
                *each(lambda n1, n2, n3: (n2, rows, WIDE)),
                dma((3,)),
                dma((8, 4)),
                dma((4,)),
                dma((4, most)),
                dma((4, 2, most)),
                dma((4, most)),
                dma((3, 2)),
                dma((3, 2)),
                dma((3, 2, most)),
                dma((3,)),
                dma((3,)),
            ],
            compiler_params=pltpu.CompilerParams(
                collective_id=0, has_side_effects=True, vmem_limit_bytes=62 * 1024 * 1024
            ),
            name="expert_backward",
        )(tokens, cotangent, route_ids, gate_probs, w_gate[0].T, w_up[0].T, w_down[0])
        return out, down[None]

    both = P(("dp", "expert"), None)
    return jax.shard_map(
        on_device,
        mesh=mesh,
        in_specs=(both, both, both, both, P("expert", None, "dp"), P("expert", None, "dp"),
                  P("expert", "dp", None)),
        out_specs=(both, P("expert", "dp", None)),
        check_vma=False,
    )


def solution(mesh):
    across = 4
    sizes = {"z": mesh.shape["dp"] // across, "x": across, "y": mesh.shape["expert"] // 2}
    return build(mesh, sizes)
```

```python
import functools

import jax
import jax.numpy as jnp
from jax import lax
from jax.experimental import pallas as pl
from jax.experimental.pallas import tpu as pltpu
from jax.sharding import PartitionSpec as P

MESH = pl.DeviceIdType.MESH
F32 = jnp.float32
BF16 = jnp.bfloat16
PIECES = 3
ROWS = 16
LANES = 128
SEGS = 8
WIDE = SEGS * LANES
ORDERS = (("y", "x", "z"), ("yz", "zy", "x"), ("z", "x", "y"), ("y", "x", "z"))
META = 3


def nearest(n):
    return sorted(range(1, n), key=lambda r: min(r, n - r))


def flat(value):
    return value.reshape(-1, value.shape[-1])


class Grid:
    def __init__(self, sizes):
        self.n = sizes
        dp, ex = lax.axis_index("dp"), lax.axis_index("expert")
        self.at = {"z": dp // sizes["x"], "x": dp % sizes["x"], "y": ex // 2}
        self.core = ex % 2
        self.sign = 1 - 2 * self.core

    def device(self, axis=None, steps=0):
        at = dict(self.at)
        core = self.core
        if axis is None:
            core = 1 - core
        elif len(axis) == 2:
            for name, here in zip(axis, (1 - core, core)):
                n = self.n[name]
                at[name] = (at[name] + self.sign * here * steps + n) % n
        else:
            n = self.n[axis]
            at[axis] = (at[axis] + self.sign * steps + n) % n
        return (at["z"] * self.n["x"] + at["x"], at["y"] * 2 + core)


def one_hot(n, source):
    out = lax.broadcasted_iota(jnp.int32, (n, n), 0)
    return (lax.broadcasted_iota(jnp.int32, (n, n), 1) == source(out)).astype(F32).astype(BF16)


def kernel(
    sizes, tok_ref, cot_ref, ids_ref, probs_ref, wg_hbm, wu_hbm, wd_hbm, out_ref, dg_ref, *scratch
):
    scratch = list(scratch)

    def take(count):
        taken = tuple(scratch[:count])
        del scratch[:count]
        return taken

    first, tiles = take(3), take(3)
    (metas,) = take(1)
    wg, wu, wd, weights = take(4)
    gate, up, grad = take(3), take(3), take(3)
    hidden, ggrad, ugrad = take(3), take(3), take(3)
    routes, sibs, lands, onces, nears = take(3), take(3), take(3), take(3), take(3)
    twices, lasts = take(3), take(3)
    (dg,) = take(1)
    opposite = take(3)
    (turns,) = take(1)
    load_sem, sent, g1_recv, g2_recv, g3_recv, s_recv = take(6)
    e_recv, o_recv, a_recv, b_recv, c_recv = take(5)

    grid = Grid(sizes)
    nz, nx, ny = sizes["z"], sizes["x"], sizes["y"]
    n1 = ny
    chips = nz * nx * ny
    other = grid.device()
    dims = [tuple(sizes[a[0]] for a in order) for order in ORDERS]

    barrier = pltpu.get_barrier_semaphore()
    around = [other]
    for axis in ("x", "y", "z"):
        around += [grid.device(axis, r) for r in range(1, sizes[axis])]
    for device in around:
        pl.semaphore_signal(barrier, inc=1, device_id=device, device_id_type=MESH)

    loads = [
        pltpu.make_async_copy(src, dst, load_sem.at[i])
        for i, (src, dst) in enumerate(((wg_hbm, wg), (wu_hbm, wu), (wd_hbm, wd)))
    ]
    for load in loads:
        load.start()

    for half, ref in enumerate((tok_ref, cot_ref)):
        value = ref[...].astype(F32)
        for p in range(PIECES):
            rows = [
                value[:, p * WIDE + s * LANES:p * WIDE + (s + 1) * LANES] for s in range(SEGS)
            ]
            first[p][0, half * ROWS:(half + 1) * ROWS] = jnp.concatenate(rows, axis=0).astype(BF16)
    lane = lax.broadcasted_iota(jnp.int32, (1, LANES), 1)
    meta = jnp.zeros((1, LANES), F32)
    for j in range(ids_ref.shape[0]):
        for k in range(ids_ref.shape[1]):
            meta = meta + jnp.where(
                lane == ids_ref[j:j + 1, k:k + 1] + 16 * j, probs_ref[j:j + 1, k:k + 1], 0.0
            )
    metas[0, 0, 0, 0] = meta
    shift = n1.bit_length() - 1
    fore = one_hot(n1 * ROWS, lambda o: (o & (n1 - 1)) * ROWS + (o >> shift))
    back = one_hot(
        n1 * ROWS, lambda o: (o & (ROWS - 1)) * n1 + (o >> 4)
    )
    span = 2 * n1 * n1
    swap = one_hot(
        span, lambda o: (o & (n1 - 1)) * 2 * n1 + ((o >> shift) & 1) * n1 + (o >> (shift + 1))
    ).astype(F32)
    same = one_hot(span, lambda o: o).astype(F32)
    for c in range(2):
        on_z = ((grid.core + c) % 2).astype(F32)
        turn = same * (1.0 - on_z) + swap * on_z
        turns[c, :, :span] = swap.astype(BF16)
        turns[c, :, span:] = turn.astype(BF16)
    pl.semaphore_wait(barrier, len(around))

    def copy_of(src, dst, ssem, rsem, device):
        return pltpu.make_async_remote_copy(
            src_ref=src, dst_ref=dst, send_sem=ssem, recv_sem=rsem,
            device_id=device, device_id_type=MESH,
        )

    def push(src, dst, kind, q, rsem, device):
        copy_of(src, dst, sent.at[kind, q], rsem, device).start()

    def arrived(dst, rsem):
        copy_of(dst, dst, sent.at[0, 0], rsem, other).wait_recv()

    def drain(ref, kind, q):
        copy_of(ref, ref, sent.at[kind, q], g1_recv.at[0], other).wait_send()

    held = [f for f in first] + [metas.at[0, 0, 0]]
    for q in range(4):
        for r in nearest(n1):
            push(held[q].at[0], held[q].at[n1 - r], 0, q, g1_recv.at[q],
                 grid.device(ORDERS[q][0], r))

    grids = list(tiles) + [metas]

    def send2(q, src, r):
        n2 = dims[q][1]
        dst = (src - r) % n2
        push(grids[q].at[0, 0, src], grids[q].at[0, 0, dst], 1, q, g2_recv.at[q, dst],
             grid.device(ORDERS[q][1], r))

    def got2(q, r):
        arrived(grids[q].at[0, 0, r], g2_recv.at[q, r])

    def one_step(q):
        return dims[q][1] <= 4

    for q in (1, 0, 2, META):
        arrived(held[q].at[pl.ds(1, n1 - 1)], g1_recv.at[q])
        if q != META:
            both = jnp.concatenate([
                first[q][:, half * ROWS:(half + 1) * ROWS].reshape(n1 * ROWS, LANES)
                for half in range(2)
            ], axis=1)
            moved = jnp.dot(fore, both, preferred_element_type=F32).astype(BF16)
            for s in range(SEGS):
                cols = slice(s * LANES, (s + 1) * LANES)
                for half in range(2):
                    tiles[q][0, 0, 0, half, :, cols] = moved[
                        s * 2 * n1:(s + 1) * 2 * n1, half * LANES:(half + 1) * LANES
                    ]
        n2 = dims[q][1]
        for r in nearest(n2):
            if one_step(q) or min(r, n2 - r) <= 2:
                send2(q, 0, r)

    def turns_of(q):
        return {0: (0, 1), 1: (0, 3, 1, 2), 2: (0, 1), META: (0,)}[q]

    have = [{0} for _ in range(4)]

    def part(q, lead, h):
        return grids[q].at[lead] if q == META else grids[q].at[lead + (pl.ds(2 * h, 2),)]

    def share(q, slot):
        ref = grids[q]
        if q != META:
            push(ref.at[0, slot], ref.at[1, slot], 3, q, s_recv.at[q, slot], other)

    def shared(q, slot):
        arrived(grids[q].at[1, slot], s_recv.at[q, slot])

    def landed(q, way, k, i):
        n3 = dims[q][2]
        turns = turns_of(q)
        slot = n3 - k if way == 0 else k
        sem = (q, way, (k - 1) * len(turns) + i)
        arrived(part(q, (0, slot), turns[i]), g3_recv.at[sem])
        if i == len(turns) - 1:
            share(q, slot)

    def second(q, r):
        if r in have[q]:
            return
        n2 = dims[q][1]
        got2(q, r)
        have[q].add(r)
        if not one_step(q):
            if r == 2:
                send2(q, 2, -1)
                send2(q, 2, -2)
            if r == n2 - 2:
                send2(q, n2 - 2, 1)

    def hop(q, k, i):
        n2, n3 = dims[q][1:]
        turns = turns_of(q)
        h = turns[i]
        if k == 1:
            for r in range(n2) if q == META else (2 * h, 2 * h + 1):
                second(q, r)
        for way in (0, 1):
            reach = n3 // 2 - way
            if 1 < k <= reach + 1:
                landed(q, way, k - 1, i)
            if k > reach:
                continue
            src = (n3 - (k - 1)) % n3 if way == 0 else k - 1
            dst = n3 - k if way == 0 else k
            sem = (q, way, (k - 1) * len(turns) + i)
            push(part(q, (0, src), h), part(q, (0, dst), h), 2, q, g3_recv.at[sem],
                 grid.device(ORDERS[q][2], 1 if way == 0 else -1))
        if k == 1 and i == len(turns) - 1:
            share(q, 0)

    across = (((1,), (1,)), ((), ()))

    def multiply(p, at):
        cols = slice(p * WIDE, (p + 1) * WIDE)
        tok = flat(tiles[p][at + (slice(None), 0)])
        cot = flat(tiles[p][at + (slice(None), 1)])
        for acc, lhs, w in ((gate, tok, wg), (up, tok, wu), (grad, cot, wd)):
            result = lax.dot_general(lhs, w[:, cols], across, preferred_element_type=F32)
            acc[p][at] = result.reshape(acc[p].at[at].shape)

    done = set()

    def use(q, slot):
        done.add((q, slot))
        if q == 1:
            shared(1, slot)
            multiply(1, (slice(None), slice(slot, slot + 1)))
        elif (q, slot ^ 1) in done:
            low = slot & ~1
            shared(q, low)
            shared(q, low + 1)
            multiply(q, (slice(None), slice(low, low + 2)))

    items = 8
    starts = ((0, 1, 4, 5), (2, 3, 6, 7))
    for tau in range(items):
        for q in (0, 2):
            hop(q, tau // 2 + 1, tau % 2)
        for k in range(2):
            for i in range(4):
                if starts[k][i] == tau:
                    hop(1, k + 1, i)
        if tau == 1:
            second(1, 2)
        if tau % 2 == 0:
            hop(META, tau // 2 + 1, 0)
        if tau == 1:
            for load in loads:
                load.wait()
        if tau % 2 == 1:
            k = tau // 2
            for q in (0, 2):
                use(q, (dims[q][2] - k) % dims[q][2])
                if 0 < k <= dims[q][2] // 2 - 1:
                    use(q, k)
        if tau == 6:
            use(1, 0)

    def weigh():
        arrived(metas.at[1], s_recv.at[META, 0])
        expert = lax.axis_index("expert")
        lane = lax.broadcasted_iota(jnp.int32, (chips, LANES), 1)
        for c in range(2):
            meta = metas[c].reshape(chips, LANES)
            halves = [
                jnp.broadcast_to(
                    jnp.sum(jnp.where(lane == j * 16 + expert, meta, 0.0), axis=1, keepdims=True),
                    (chips, LANES),
                )
                for j in range(2)
            ]
            for j in range(2):
                weights[c, :, :, j] = halves[j].reshape(nz, nx, ny, LANES)

    for slot in range(1, nx):
        if slot != nx // 2:
            use(1, slot)
    landed(META, 0, nz // 2, 0)
    push(metas.at[0], metas.at[1], 3, META, s_recv.at[META, 0], other)
    weigh()
    for q in (0, 2):
        for i in range(len(turns_of(q))):
            landed(q, 0, dims[q][2] // 2, i)
    for q in (0, 2):
        use(q, dims[q][2] // 2)
    for i in range(len(turns_of(1))):
        landed(1, 0, nx // 2, i)
    use(1, nx // 2)

    def activate(i, _):
        c, x = i // nx, i % nx
        both = turns[c]
        sums = []
        for acc in (gate, up, grad):
            value = jnp.concatenate([flat(acc[2][c, :, x]), flat(acc[1][c, x])], axis=0)
            high = value.astype(BF16)
            low = (value - high.astype(F32)).astype(BF16)
            sums.append(
                flat(acc[0][c, :, x]) + jnp.dot(both, high, preferred_element_type=F32)
                + jnp.dot(both, low, preferred_element_type=F32)
            )
        gate_pre, up_pre, down = sums
        weight = flat(weights[c, :, x])[:, 0:1]
        down = down * weight
        sigma = jax.nn.sigmoid(gate_pre)
        active = gate_pre * sigma
        slope = sigma * (1.0 + gate_pre * (1.0 - sigma))
        for ref, value in (
            (hidden, active * up_pre * weight), (ggrad, down * up_pre * slope), (ugrad, down * active)
        ):
            value = value.astype(BF16)
            shape = ref[1].shape[2:]
            ref[0][c, :, x] = value.reshape(shape)
            for p, at in ((1, (c, x)), (2, (c, slice(None), x))):
                turn = both[:, :span] if p == 2 else both[:, span:]
                moved = jnp.dot(turn, value, preferred_element_type=F32).astype(BF16)
                ref[p][at] = moved.reshape(shape)
        return 0

    for i in range(2 * nx):
        activate(i, 0)

    def expand(p, c, half):
        cols = slice(p * WIDE, (p + 1) * WIDE)
        n3 = dims[p][2]
        rows = (c, slice(half * n3 // 2, (half + 1) * n3 // 2))
        term = jnp.dot(flat(ggrad[p][rows]), wg[:, cols], preferred_element_type=F32)
        term = term + jnp.dot(flat(ugrad[p][rows]), wu[:, cols], preferred_element_type=F32)
        routes[p][rows] = term.astype(BF16).reshape(routes[p].at[rows].shape)

    def total(dst, terms, indices):
        for index in indices:
            value = terms[0][index].astype(F32)
            for term in terms[1:]:
                value = value + term[index].astype(F32)
            dst[index] = value.astype(BF16)

    def reach_of(p, way):
        n3 = dims[p][2]
        return 3 if n3 == 8 else n3 // 2 - way

    def reduce_hop(p, t, h):
        n2, n3 = dims[p][1:]
        rows, some = (2 * h, 2 * h + 1), pl.ds(2 * h, 2)
        parts = n2 // 2
        if t == 1 and n3 == 8:
            theirs = sibs[p].at[4]
            total(theirs, [routes[p].at[0, 4], theirs], rows)
            push(theirs.at[some], opposite[p].at[some], 5, p, o_recv.at[p, h],
                 grid.device(ORDERS[p][2], -2))
        for way in (0, 1):
            reach = reach_of(p, way)
            if t > reach:
                continue
            d = reach + 1 - t
            slot = n3 - d if way == 0 else d
            mine, theirs = routes[p].at[0, slot], sibs[p].at[slot]
            sem = (p, way, (t - 1) * parts + h)
            if t == 1:
                total(theirs, [mine, theirs], rows)
                src = theirs.at[some]
            else:
                land = lands[p].at[way, t - 2]
                src = land.at[some]
                terms = [land, mine, theirs]
                if n3 == 8 and t == 2 and way == 0:
                    arrived(opposite[p].at[some], o_recv.at[p, h])
                    terms.append(opposite[p])
                arrived(src, a_recv.at[p, way, (t - 2) * parts + h])
                total(land, terms, rows)
            push(src, lands[p].at[way, t - 1, some], 5, p, a_recv.at[sem],
                 grid.device(ORDERS[p][2], -1 if way == 0 else 1))

    chunk = WIDE // 2

    def descend(p, half):
        cols = slice(p * WIDE + half * chunk, p * WIDE + (half + 1) * chunk)
        rhs = tiles[p][:, :, :, 1, :, half * chunk:(half + 1) * chunk]
        dg[:, cols] = lax.dot_general(
            flat(hidden[p][...]), flat(rhs), (((0,), (0,)), ((), ())), preferred_element_type=F32
        ).astype(BF16)

    def hand_over(p):
        n3 = dims[p][2]
        for half in (1, 0):
            expand(p, 1, half)
            some = pl.ds(half * n3 // 2, n3 // 2)
            push(routes[p].at[1, some], sibs[p].at[some], 4, p, e_recv.at[p, half], other)

    def set_out(p):
        n3 = dims[p][2]
        for half in (1, 0):
            expand(p, 0, half)
        for half in (1, 0):
            some = pl.ds(half * n3 // 2, n3 // 2)
            arrived(sibs[p].at[some], e_recv.at[p, half])
        for h in range(dims[p][1] // 2):
            reduce_hop(p, 1, h)

    def settle(p, h):
        n2, n3 = dims[p][1:]
        rows, some = (2 * h, 2 * h + 1), pl.ds(2 * h, 2)
        terms = [routes[p].at[0, 0], sibs[p].at[0]]
        for way in (0, 1):
            reach = reach_of(p, way)
            land = lands[p].at[way, reach - 1]
            arrived(land.at[some], a_recv.at[p, way, (reach - 1) * (n2 // 2) + h])
            terms.append(land)
        total(onces[p], terms, rows)
        for r in rows:
            if r > 0:
                push(onces[p].at[r], nears[p].at[r - 1], 6, p, b_recv.at[p],
                     grid.device(ORDERS[p][1], r))

    hand_over(1)
    hand_over(0)
    set_out(1)
    hand_over(2)
    set_out(0)
    set_out(2)
    for tau in range(2, 6):
        for p in (0, 2):
            reduce_hop(p, tau // 2 + 1, tau % 2)
        if tau == 3:
            for p in range(PIECES):
                descend(p, 0)
        if tau in (3, 4):
            for h in (2 * tau - 6, 2 * tau - 5):
                reduce_hop(1, 2, h)
    for h in range(4):
        settle(1, h)
    for p in range(PIECES):
        descend(p, 1)
    store = pltpu.make_async_copy(dg, dg_ref, load_sem.at[0])
    store.start()
    for h in (0, 1):
        for p in (0, 2):
            settle(p, h)

    order = (0, 2, 1)
    for p in order:
        n2 = dims[p][1]
        value = onces[p][0].astype(F32)
        arrived(nears[p], b_recv.at[p])
        for r in nearest(n2):
            value = value + nears[p][r - 1].astype(F32)
        value = value.astype(BF16)
        stack = jnp.concatenate(
            [value[:, s * LANES:(s + 1) * LANES] for s in range(SEGS)], axis=0
        )
        moved = jnp.dot(back, stack, preferred_element_type=F32).astype(BF16)
        twices[p][...] = moved.reshape(n1, ROWS, LANES)
        for r in nearest(n1):
            push(twices[p].at[r], lasts[p].at[r - 1], 7, p, c_recv.at[p],
                 grid.device(ORDERS[p][0], r))
    for p in order:
        value = twices[p][0].astype(F32)
        arrived(lasts[p], c_recv.at[p])
        for r in nearest(n1):
            value = value + lasts[p][r - 1].astype(F32)
        count = out_ref.shape[0]
        for s in range(SEGS):
            cols = slice(p * WIDE + s * LANES, p * WIDE + (s + 1) * LANES)
            out_ref[:, cols] = value[s * count:(s + 1) * count].astype(BF16)

    for q in range(4):
        n2, n3 = dims[q][1:]
        drain(held[q].at[pl.ds(0, n1 - 1)], 0, q)
        drain(grids[q].at[0, 0, pl.ds(0, n2 - 1)], 1, q)
        drain(grids[q].at[0, pl.ds(0, n3 - 1)], 2, q)
        drain(grids[q].at[0], 3, q)
    for p in range(PIECES):
        n2, n3 = dims[p][1:]
        drain(routes[p].at[1], 4, p)
        drain(sibs[p].at[pl.ds(0, n3 - 1)], 5, p)
        drain(onces[p].at[pl.ds(0, n2 - 1)], 6, p)
        drain(twices[p].at[pl.ds(0, n1 - 1)], 7, p)
    store.wait()


def build(mesh, sizes):
    nz, nx, ny = sizes["z"], sizes["x"], sizes["y"]
    assert ny == nz

    def on_device(tokens, cotangent, route_ids, gate_probs, w_gate, w_up, w_down):
        count, width = tokens.shape
        hid = w_gate.shape[2]
        n = [tuple(sizes[a[0]] for a in order) for order in ORDERS]
        vm = pl.BlockSpec(memory_space=pltpu.VMEM)
        hbm = pl.BlockSpec(memory_space=pl.ANY)
        dma = pltpu.SemaphoreType.DMA
        rows = 2 * ny

        def each(shape_of, dtype=BF16):
            return [pltpu.VMEM(shape_of(*n[p]), dtype) for p in range(PIECES)]

        def sums(dtype):
            return each(lambda n1, n2, n3: (2, n3, n2, rows, hid), dtype)

        most = max(nz, ny, nx)
        out, down = pl.pallas_call(
            functools.partial(kernel, sizes),
            out_shape=(
                jax.ShapeDtypeStruct((count, width), BF16),
                jax.ShapeDtypeStruct((hid, width), BF16),
            ),
            in_specs=[vm, vm, vm, vm, hbm, hbm, hbm],
            out_specs=(vm, hbm),
            scratch_shapes=[
                *each(lambda n1, n2, n3: (n1, 2 * ROWS, LANES)),
                *each(lambda n1, n2, n3: (2, n3, n2, 2, rows, WIDE)),
                pltpu.VMEM((2, nz, nx, ny, 1, LANES), F32),
                *[pltpu.VMEM((hid, width), BF16) for _ in range(3)],
                pltpu.VMEM((2, nz, nx, 2, ny, LANES), F32),
                *sums(F32), *sums(F32), *sums(F32),
                *sums(BF16), *sums(BF16), *sums(BF16),
                *each(lambda n1, n2, n3: (2, n3, n2, rows, WIDE)),
                *each(lambda n1, n2, n3: (n3, n2, rows, WIDE)),
                *each(lambda n1, n2, n3: (2, n3 // 2, n2, rows, WIDE)),
                *each(lambda n1, n2, n3: (n2, rows, WIDE)),
                *each(lambda n1, n2, n3: (n2 - 1, rows, WIDE)),
                *each(lambda n1, n2, n3: (n1, ROWS, LANES)),
                *each(lambda n1, n2, n3: (n1 - 1, ROWS, LANES)),
                pltpu.VMEM((hid, width), BF16),
                *each(lambda n1, n2, n3: (n2, rows, WIDE)),
                pltpu.VMEM((2, rows * nz, 2 * rows * nz), BF16),
                dma((3,)),
                dma((8, 4)),
                dma((4,)),
                dma((4, most)),
                dma((4, 2, most)),
                dma((4, most)),
                dma((3, 2)),
                dma((3, 2)),
                dma((3, 2, most)),
                dma((3,)),
                dma((3,)),
            ],
            compiler_params=pltpu.CompilerParams(
                collective_id=0, has_side_effects=True, vmem_limit_bytes=62 * 1024 * 1024
            ),
            name="expert_backward",
        )(tokens, cotangent, route_ids, gate_probs, w_gate[0].T, w_up[0].T, w_down[0])
        return out, down[None]

    both = P(("dp", "expert"), None)
    return jax.shard_map(
        on_device,
        mesh=mesh,
        in_specs=(both, both, both, both, P("expert", None, "dp"), P("expert", None, "dp"),
                  P("expert", "dp", None)),
        out_specs=(both, P("expert", "dp", None)),
        check_vma=False,
    )


def solution(mesh):
    across = 4
    sizes = {"z": mesh.shape["dp"] // across, "x": across, "y": mesh.shape["expert"] // 2}
    return build(mesh, sizes)
```

```python
import functools

import jax
import jax.numpy as jnp
from jax import lax
from jax.experimental import pallas as pl
from jax.experimental.pallas import tpu as pltpu
from jax.sharding import PartitionSpec as P

MESH = pl.DeviceIdType.MESH
F32 = jnp.float32
BF16 = jnp.bfloat16
PIECES = 3
ROWS = 16
LANES = 128
SEGS = 8
WIDE = SEGS * LANES
ORDERS = (("y", "x", "z"), ("yz", "zy", "x"), ("z", "x", "y"), ("y", "x", "z"))
META = 3


def nearest(n):
    return sorted(range(1, n), key=lambda r: min(r, n - r))


def flat(value):
    return value.reshape(-1, value.shape[-1])


class Grid:
    def __init__(self, sizes):
        self.n = sizes
        dp, ex = lax.axis_index("dp"), lax.axis_index("expert")
        self.at = {"z": dp // sizes["x"], "x": dp % sizes["x"], "y": ex // 2}
        self.core = ex % 2
        self.sign = 1 - 2 * self.core

    def device(self, axis=None, steps=0):
        at = dict(self.at)
        core = self.core
        if axis is None:
            core = 1 - core
        elif len(axis) == 2:
            for name, here in zip(axis, (1 - core, core)):
                n = self.n[name]
                at[name] = (at[name] + self.sign * here * steps + n) % n
        else:
            n = self.n[axis]
            at[axis] = (at[axis] + self.sign * steps + n) % n
        return (at["z"] * self.n["x"] + at["x"], at["y"] * 2 + core)


def one_hot(n, source):
    out = lax.broadcasted_iota(jnp.int32, (n, n), 0)
    return (lax.broadcasted_iota(jnp.int32, (n, n), 1) == source(out)).astype(F32).astype(BF16)


def kernel(
    sizes, tok_ref, cot_ref, ids_ref, probs_ref, wg_hbm, wu_hbm, wd_hbm, out_ref, dg_ref, *scratch
):
    scratch = list(scratch)

    def take(count):
        taken = tuple(scratch[:count])
        del scratch[:count]
        return taken

    first, tiles = take(3), take(3)
    (metas,) = take(1)
    wg, wu, wd, weights = take(4)
    gate, up, grad = take(3), take(3), take(3)
    hidden, ggrad, ugrad = take(3), take(3), take(3)
    routes, sibs, lands, onces, nears = take(3), take(3), take(3), take(3), take(3)
    twices, lasts = take(3), take(3)
    (dg,) = take(1)
    opposite = take(3)
    (turns,) = take(1)
    load_sem, sent, g1_recv, g2_recv, g3_recv, s_recv = take(6)
    e_recv, o_recv, a_recv, b_recv, c_recv = take(5)

    grid = Grid(sizes)
    nz, nx, ny = sizes["z"], sizes["x"], sizes["y"]
    n1 = ny
    chips = nz * nx * ny
    other = grid.device()
    dims = [tuple(sizes[a[0]] for a in order) for order in ORDERS]

    barrier = pltpu.get_barrier_semaphore()
    around = [other]
    for axis in ("x", "y", "z"):
        around += [grid.device(axis, r) for r in range(1, sizes[axis])]
    for device in around:
        pl.semaphore_signal(barrier, inc=1, device_id=device, device_id_type=MESH)

    loads = [
        pltpu.make_async_copy(src, dst, load_sem.at[i])
        for i, (src, dst) in enumerate(((wg_hbm, wg), (wu_hbm, wu), (wd_hbm, wd)))
    ]
    for load in loads:
        load.start()

    for half, ref in enumerate((tok_ref, cot_ref)):
        value = ref[...].astype(F32)
        for p in range(PIECES):
            rows = [
                value[:, p * WIDE + s * LANES:p * WIDE + (s + 1) * LANES] for s in range(SEGS)
            ]
            first[p][0, half * ROWS:(half + 1) * ROWS] = jnp.concatenate(rows, axis=0).astype(BF16)
    lane = lax.broadcasted_iota(jnp.int32, (1, LANES), 1)
    meta = jnp.zeros((1, LANES), F32)
    for j in range(ids_ref.shape[0]):
        for k in range(ids_ref.shape[1]):
            meta = meta + jnp.where(
                lane == ids_ref[j:j + 1, k:k + 1] + 16 * j, probs_ref[j:j + 1, k:k + 1], 0.0
            )
    metas[0, 0, 0, 0] = meta
    shift = n1.bit_length() - 1
    fore = one_hot(n1 * ROWS, lambda o: (o & (n1 - 1)) * ROWS + (o >> shift))
    back = one_hot(
        n1 * ROWS, lambda o: (o & (ROWS - 1)) * n1 + (o >> 4)
    )
    span = 2 * n1 * n1
    swap = one_hot(
        span, lambda o: (o & (n1 - 1)) * 2 * n1 + ((o >> shift) & 1) * n1 + (o >> (shift + 1))
    ).astype(F32)
    same = one_hot(span, lambda o: o).astype(F32)
    for c in range(2):
        on_z = ((grid.core + c) % 2).astype(F32)
        turn = same * (1.0 - on_z) + swap * on_z
        turns[c, :, :span] = swap.astype(BF16)
        turns[c, :, span:] = turn.astype(BF16)
    pl.semaphore_wait(barrier, len(around))

    def copy_of(src, dst, ssem, rsem, device):
        return pltpu.make_async_remote_copy(
            src_ref=src, dst_ref=dst, send_sem=ssem, recv_sem=rsem,
            device_id=device, device_id_type=MESH,
        )

    def push(src, dst, kind, q, rsem, device):
        copy_of(src, dst, sent.at[kind, q], rsem, device).start()

    def arrived(dst, rsem):
        copy_of(dst, dst, sent.at[0, 0], rsem, other).wait_recv()

    def drain(ref, kind, q):
        copy_of(ref, ref, sent.at[kind, q], g1_recv.at[0], other).wait_send()

    held = [f for f in first] + [metas.at[0, 0, 0]]
    for q in range(4):
        for r in nearest(n1):
            push(held[q].at[0], held[q].at[n1 - r], 0, q, g1_recv.at[q],
                 grid.device(ORDERS[q][0], r))

    grids = list(tiles) + [metas]

    def send2(q, src, r):
        n2 = dims[q][1]
        dst = (src - r) % n2
        push(grids[q].at[0, 0, src], grids[q].at[0, 0, dst], 1, q, g2_recv.at[q, dst],
             grid.device(ORDERS[q][1], r))

    def got2(q, r):
        arrived(grids[q].at[0, 0, r], g2_recv.at[q, r])

    def one_step(q):
        return dims[q][1] <= 4

    for q in (1, 0, 2, META):
        arrived(held[q].at[pl.ds(1, n1 - 1)], g1_recv.at[q])
        if q != META:
            both = jnp.concatenate([
                first[q][:, half * ROWS:(half + 1) * ROWS].reshape(n1 * ROWS, LANES)
                for half in range(2)
            ], axis=1)
            moved = jnp.dot(fore, both, preferred_element_type=F32).astype(BF16)
            for s in range(SEGS):
                cols = slice(s * LANES, (s + 1) * LANES)
                for half in range(2):
                    tiles[q][0, 0, 0, half, :, cols] = moved[
                        s * 2 * n1:(s + 1) * 2 * n1, half * LANES:(half + 1) * LANES
                    ]
        n2 = dims[q][1]
        for r in nearest(n2):
            if one_step(q) or min(r, n2 - r) <= 2:
                send2(q, 0, r)

    def turns_of(q):
        return {0: (0, 1), 1: (0, 3, 1, 2), 2: (0, 1), META: (0,)}[q]

    have = [{0} for _ in range(4)]

    def part(q, lead, h):
        return grids[q].at[lead] if q == META else grids[q].at[lead + (pl.ds(2 * h, 2),)]

    def share(q, slot):
        ref = grids[q]
        if q != META:
            push(ref.at[0, slot], ref.at[1, slot], 3, q, s_recv.at[q, slot], other)

    def shared(q, slot):
        arrived(grids[q].at[1, slot], s_recv.at[q, slot])

    def landed(q, way, k, i):
        n3 = dims[q][2]
        turns = turns_of(q)
        slot = n3 - k if way == 0 else k
        sem = (q, way, (k - 1) * len(turns) + i)
        arrived(part(q, (0, slot), turns[i]), g3_recv.at[sem])
        if i == len(turns) - 1:
            share(q, slot)

    def second(q, r):
        if r in have[q]:
            return
        n2 = dims[q][1]
        got2(q, r)
        have[q].add(r)
        if not one_step(q):
            if r == 2:
                send2(q, 2, -1)
                send2(q, 2, -2)
            if r == n2 - 2:
                send2(q, n2 - 2, 1)

    def hop(q, k, i):
        n2, n3 = dims[q][1:]
        turns = turns_of(q)
        h = turns[i]
        if k == 1:
            for r in range(n2) if q == META else (2 * h, 2 * h + 1):
                second(q, r)
        for way in (0, 1):
            reach = n3 // 2 - way
            if 1 < k <= reach + 1:
                landed(q, way, k - 1, i)
            if k > reach:
                continue
            src = (n3 - (k - 1)) % n3 if way == 0 else k - 1
            dst = n3 - k if way == 0 else k
            sem = (q, way, (k - 1) * len(turns) + i)
            push(part(q, (0, src), h), part(q, (0, dst), h), 2, q, g3_recv.at[sem],
                 grid.device(ORDERS[q][2], 1 if way == 0 else -1))
        if k == 1 and i == len(turns) - 1:
            share(q, 0)

    across = (((1,), (1,)), ((), ()))

    def multiply(p, at):
        cols = slice(p * WIDE, (p + 1) * WIDE)
        tok = flat(tiles[p][at + (slice(None), 0)])
        cot = flat(tiles[p][at + (slice(None), 1)])
        for acc, lhs, w in ((gate, tok, wg), (up, tok, wu), (grad, cot, wd)):
            result = lax.dot_general(lhs, w[:, cols], across, preferred_element_type=F32)
            acc[p][at] = result.reshape(acc[p].at[at].shape)

    done = set()

    def use(q, slot):
        done.add((q, slot))
        if q == 1:
            shared(1, slot)
            multiply(1, (slice(None), slice(slot, slot + 1)))
        elif (q, slot ^ 1) in done:
            low = slot & ~1
            shared(q, low)
            shared(q, low + 1)
            multiply(q, (slice(None), slice(low, low + 2)))

    items = 8
    starts = ((0, 1, 4, 5), (2, 3, 6, 7))
    for tau in range(items):
        for q in (0, 2):
            hop(q, tau // 2 + 1, tau % 2)
        for k in range(2):
            for i in range(4):
                if starts[k][i] == tau:
                    hop(1, k + 1, i)
        if tau == 1:
            second(1, 2)
        if tau % 2 == 0:
            hop(META, tau // 2 + 1, 0)
        if tau == 1:
            for load in loads:
                load.wait()
        if tau % 2 == 1:
            k = tau // 2
            for q in (0, 2):
                use(q, (dims[q][2] - k) % dims[q][2])
                if 0 < k <= dims[q][2] // 2 - 1:
                    use(q, k)
        if tau == 6:
            use(1, 0)

    def weigh():
        arrived(metas.at[1], s_recv.at[META, 0])
        expert = lax.axis_index("expert")
        lane = lax.broadcasted_iota(jnp.int32, (chips, LANES), 1)
        for c in range(2):
            meta = metas[c].reshape(chips, LANES)
            halves = [
                jnp.broadcast_to(
                    jnp.sum(jnp.where(lane == j * 16 + expert, meta, 0.0), axis=1, keepdims=True),
                    (chips, LANES),
                )
                for j in range(2)
            ]
            for j in range(2):
                weights[c, :, :, j] = halves[j].reshape(nz, nx, ny, LANES)

    for slot in range(1, nx):
        if slot != nx // 2:
            use(1, slot)
    landed(META, 0, nz // 2, 0)
    push(metas.at[0], metas.at[1], 3, META, s_recv.at[META, 0], other)
    weigh()
    for q in (0, 2):
        for i in range(len(turns_of(q))):
            landed(q, 0, dims[q][2] // 2, i)
    for q in (0, 2):
        use(q, dims[q][2] // 2)
    for i in range(len(turns_of(1))):
        landed(1, 0, nx // 2, i)
    use(1, nx // 2)

    def activate(i, _):
        c, x = i // nx, i % nx
        both = turns[c]
        sums = []
        for acc in (gate, up, grad):
            value = jnp.concatenate([flat(acc[2][c, :, x]), flat(acc[1][c, x])], axis=0)
            high = value.astype(BF16)
            low = (value - high.astype(F32)).astype(BF16)
            sums.append(
                flat(acc[0][c, :, x]) + jnp.dot(both, high, preferred_element_type=F32)
                + jnp.dot(both, low, preferred_element_type=F32)
            )
        gate_pre, up_pre, down = sums
        weight = flat(weights[c, :, x])[:, 0:1]
        down = down * weight
        sigma = jax.nn.sigmoid(gate_pre)
        active = gate_pre * sigma
        slope = sigma * (1.0 + gate_pre * (1.0 - sigma))
        for ref, value in (
            (hidden, active * up_pre * weight), (ggrad, down * up_pre * slope), (ugrad, down * active)
        ):
            value = value.astype(BF16)
            shape = ref[1].shape[2:]
            ref[0][c, :, x] = value.reshape(shape)
            for p, at in ((1, (c, x)), (2, (c, slice(None), x))):
                turn = both[:, :span] if p == 2 else both[:, span:]
                moved = jnp.dot(turn, value, preferred_element_type=F32).astype(BF16)
                ref[p][at] = moved.reshape(shape)
        return 0

    for i in range(2 * nx):
        activate(i, 0)

    def expand(p, c, half):
        cols = slice(p * WIDE, (p + 1) * WIDE)
        n3 = dims[p][2]
        rows = (c, slice(half * n3 // 2, (half + 1) * n3 // 2))
        term = jnp.dot(flat(ggrad[p][rows]), wg[:, cols], preferred_element_type=F32)
        term = term + jnp.dot(flat(ugrad[p][rows]), wu[:, cols], preferred_element_type=F32)
        routes[p][rows] = term.astype(BF16).reshape(routes[p].at[rows].shape)

    def total(dst, terms, indices):
        for index in indices:
            value = terms[0][index].astype(F32)
            for term in terms[1:]:
                value = value + term[index].astype(F32)
            dst[index] = value.astype(BF16)

    def reach_of(p, way):
        n3 = dims[p][2]
        return 3 if n3 == 8 else n3 // 2 - way

    def reduce_hop(p, t, h):
        n2, n3 = dims[p][1:]
        rows, some = (2 * h, 2 * h + 1), pl.ds(2 * h, 2)
        parts = n2 // 2
        if t == 1 and n3 == 8:
            theirs = sibs[p].at[4]
            total(theirs, [routes[p].at[0, 4], theirs], rows)
            push(theirs.at[some], opposite[p].at[some], 5, p, o_recv.at[p, h],
                 grid.device(ORDERS[p][2], -2))
        for way in (0, 1):
            reach = reach_of(p, way)
            if t > reach:
                continue
            d = reach + 1 - t
            slot = n3 - d if way == 0 else d
            mine, theirs = routes[p].at[0, slot], sibs[p].at[slot]
            sem = (p, way, (t - 1) * parts + h)
            if t == 1:
                total(theirs, [mine, theirs], rows)
                src = theirs.at[some]
            else:
                land = lands[p].at[way, t - 2]
                src = land.at[some]
                terms = [land, mine, theirs]
                if n3 == 8 and t == 2 and way == 0:
                    arrived(opposite[p].at[some], o_recv.at[p, h])
                    terms.append(opposite[p])
                arrived(src, a_recv.at[p, way, (t - 2) * parts + h])
                total(land, terms, rows)
            push(src, lands[p].at[way, t - 1, some], 5, p, a_recv.at[sem],
                 grid.device(ORDERS[p][2], -1 if way == 0 else 1))

    chunk = WIDE // 2

    def descend(p, half):
        cols = slice(p * WIDE + half * chunk, p * WIDE + (half + 1) * chunk)
        rhs = tiles[p][:, :, :, 1, :, half * chunk:(half + 1) * chunk]
        dg[:, cols] = lax.dot_general(
            flat(hidden[p][...]), flat(rhs), (((0,), (0,)), ((), ())), preferred_element_type=F32
        ).astype(BF16)

    def hand_over(p):
        n3 = dims[p][2]
        for half in (1, 0):
            expand(p, 1, half)
            some = pl.ds(half * n3 // 2, n3 // 2)
            push(routes[p].at[1, some], sibs[p].at[some], 4, p, e_recv.at[p, half], other)

    def set_out(p):
        n3 = dims[p][2]
        for half in (1, 0):
            expand(p, 0, half)
        for half in (1, 0):
            some = pl.ds(half * n3 // 2, n3 // 2)
            arrived(sibs[p].at[some], e_recv.at[p, half])
        for h in range(dims[p][1] // 2):
            reduce_hop(p, 1, h)

    def settle(p, h):
        n2, n3 = dims[p][1:]
        rows, some = (2 * h, 2 * h + 1), pl.ds(2 * h, 2)
        terms = [routes[p].at[0, 0], sibs[p].at[0]]
        for way in (0, 1):
            reach = reach_of(p, way)
            land = lands[p].at[way, reach - 1]
            arrived(land.at[some], a_recv.at[p, way, (reach - 1) * (n2 // 2) + h])
            terms.append(land)
        total(onces[p], terms, rows)
        for r in rows:
            if r > 0:
                push(onces[p].at[r], nears[p].at[r - 1], 6, p, b_recv.at[p],
                     grid.device(ORDERS[p][1], r))

    hand_over(0)
    hand_over(2)
    set_out(0)
    hand_over(1)
    set_out(2)
    set_out(1)
    for tau in range(2, 6):
        for p in (0, 2):
            reduce_hop(p, tau // 2 + 1, tau % 2)
        if tau == 3:
            for p in range(PIECES):
                descend(p, 0)
        if tau in (3, 4):
            for h in (2 * tau - 6, 2 * tau - 5):
                reduce_hop(1, 2, h)
    for h in range(4):
        settle(1, h)
    for h in (0, 1):
        for p in (0, 2):
            settle(p, h)
    for p in range(PIECES):
        descend(p, 1)
    store = pltpu.make_async_copy(dg, dg_ref, load_sem.at[0])
    store.start()

    order = (0, 2, 1)
    for p in order:
        n2 = dims[p][1]
        value = onces[p][0].astype(F32)
        arrived(nears[p], b_recv.at[p])
        for r in nearest(n2):
            value = value + nears[p][r - 1].astype(F32)
        value = value.astype(BF16)
        stack = jnp.concatenate(
            [value[:, s * LANES:(s + 1) * LANES] for s in range(SEGS)], axis=0
        )
        moved = jnp.dot(back, stack, preferred_element_type=F32).astype(BF16)
        twices[p][...] = moved.reshape(n1, ROWS, LANES)
        for r in nearest(n1):
            push(twices[p].at[r], lasts[p].at[r - 1], 7, p, c_recv.at[p],
                 grid.device(ORDERS[p][0], r))
    for p in order:
        value = twices[p][0].astype(F32)
        arrived(lasts[p], c_recv.at[p])
        for r in nearest(n1):
            value = value + lasts[p][r - 1].astype(F32)
        count = out_ref.shape[0]
        for s in range(SEGS):
            cols = slice(p * WIDE + s * LANES, p * WIDE + (s + 1) * LANES)
            out_ref[:, cols] = value[s * count:(s + 1) * count].astype(BF16)

    for q in range(4):
        n2, n3 = dims[q][1:]
        drain(held[q].at[pl.ds(0, n1 - 1)], 0, q)
        drain(grids[q].at[0, 0, pl.ds(0, n2 - 1)], 1, q)
        drain(grids[q].at[0, pl.ds(0, n3 - 1)], 2, q)
        drain(grids[q].at[0], 3, q)
    for p in range(PIECES):
        n2, n3 = dims[p][1:]
        drain(routes[p].at[1], 4, p)
        drain(sibs[p].at[pl.ds(0, n3 - 1)], 5, p)
        drain(onces[p].at[pl.ds(0, n2 - 1)], 6, p)
        drain(twices[p].at[pl.ds(0, n1 - 1)], 7, p)
    store.wait()


def build(mesh, sizes):
    nz, nx, ny = sizes["z"], sizes["x"], sizes["y"]
    assert ny == nz

    def on_device(tokens, cotangent, route_ids, gate_probs, w_gate, w_up, w_down):
        count, width = tokens.shape
        hid = w_gate.shape[2]
        n = [tuple(sizes[a[0]] for a in order) for order in ORDERS]
        vm = pl.BlockSpec(memory_space=pltpu.VMEM)
        hbm = pl.BlockSpec(memory_space=pl.ANY)
        dma = pltpu.SemaphoreType.DMA
        rows = 2 * ny

        def each(shape_of, dtype=BF16):
            return [pltpu.VMEM(shape_of(*n[p]), dtype) for p in range(PIECES)]

        def sums(dtype):
            return each(lambda n1, n2, n3: (2, n3, n2, rows, hid), dtype)

        most = max(nz, ny, nx)
        out, down = pl.pallas_call(
            functools.partial(kernel, sizes),
            out_shape=(
                jax.ShapeDtypeStruct((count, width), BF16),
                jax.ShapeDtypeStruct((hid, width), BF16),
            ),
            in_specs=[vm, vm, vm, vm, hbm, hbm, hbm],
            out_specs=(vm, hbm),
            scratch_shapes=[
                *each(lambda n1, n2, n3: (n1, 2 * ROWS, LANES)),
                *each(lambda n1, n2, n3: (2, n3, n2, 2, rows, WIDE)),
                pltpu.VMEM((2, nz, nx, ny, 1, LANES), F32),
                *[pltpu.VMEM((hid, width), BF16) for _ in range(3)],
                pltpu.VMEM((2, nz, nx, 2, ny, LANES), F32),
                *sums(F32), *sums(F32), *sums(F32),
                *sums(BF16), *sums(BF16), *sums(BF16),
                *each(lambda n1, n2, n3: (2, n3, n2, rows, WIDE)),
                *each(lambda n1, n2, n3: (n3, n2, rows, WIDE)),
                *each(lambda n1, n2, n3: (2, n3 // 2, n2, rows, WIDE)),
                *each(lambda n1, n2, n3: (n2, rows, WIDE)),
                *each(lambda n1, n2, n3: (n2 - 1, rows, WIDE)),
                *each(lambda n1, n2, n3: (n1, ROWS, LANES)),
                *each(lambda n1, n2, n3: (n1 - 1, ROWS, LANES)),
                pltpu.VMEM((hid, width), BF16),
                *each(lambda n1, n2, n3: (n2, rows, WIDE)),
                pltpu.VMEM((2, rows * nz, 2 * rows * nz), BF16),
                dma((3,)),
                dma((8, 4)),
                dma((4,)),
                dma((4, most)),
                dma((4, 2, most)),
                dma((4, most)),
                dma((3, 2)),
                dma((3, 2)),
                dma((3, 2, most)),
                dma((3,)),
                dma((3,)),
            ],
            compiler_params=pltpu.CompilerParams(
                collective_id=0, has_side_effects=True, vmem_limit_bytes=62 * 1024 * 1024
            ),
            name="expert_backward",
        )(tokens, cotangent, route_ids, gate_probs, w_gate[0].T, w_up[0].T, w_down[0])
        return out, down[None]

    both = P(("dp", "expert"), None)
    return jax.shard_map(
        on_device,
        mesh=mesh,
        in_specs=(both, both, both, both, P("expert", None, "dp"), P("expert", None, "dp"),
                  P("expert", "dp", None)),
        out_specs=(both, P("expert", "dp", None)),
        check_vma=False,
    )


def solution(mesh):
    across = 4
    sizes = {"z": mesh.shape["dp"] // across, "x": across, "y": mesh.shape["expert"] // 2}
    return build(mesh, sizes)
```
